512 devices in a mesh: seq: 64 (over z, x), tp: 8 (over y, core).
Axes of the slice: x: 4, y: 4, z: 16, core: 2. Of those that a mesh axis runs over, the one named last changes fastest.
Arguments:
- prefill_hidden: bfloat16 [8192, 5120], P('seq', 'tp'), may hold values from -14 to 14
- prefill_query_rows: bfloat16 [8192, 5120], P('seq', 'tp'), may hold values from -250 to 250
- prefill_key_value: bfloat16 [2, 8192, 1024], P(None, 'seq', 'tp'), may hold values from -5 to 5
- request_prefix_cache: bfloat16 [2, 64, 768, 1024], P(None, 'seq', None, 'tp'), may hold values from -5 to 5
- prefix_lengths: int32 [64], replicated, may hold values from 0 to 768, as said below
- decode_hidden: bfloat16 [4, 5120], P(None, 'tp'), may hold values from -14 to 14
- decode_query_rows: bfloat16 [4, 5120], P(None, 'tp'), may hold values from -250 to 250
- decode_kv: bfloat16 [2, 4, 1024], P(None, None, 'tp'), may hold values from -5 to 5
- decode_slot_cache: bfloat16 [2, 5, 8192, 1024], P(None, None, 'seq', 'tp'), may hold values from -5 to 5
- cache_lengths: int32 [4], replicated, may hold values from 2048 to 8192, as said below
- slot_table: int32 [4], replicated, may hold values from 0 to 4, as said below
- out_weight: bfloat16 [5120, 5120], P('tp', 'seq'), may hold values from -0.078125 to 0.078125
- final_gain: bfloat16 [5120], replicated, may hold values from 0.5 to 1.5
- head_weight: bfloat16 [5120, 152064], P(None, ('seq', 'tp')), may hold values from -4 to 4
Outputs:
- prefill_out: bfloat16 [8192, 5120], P('seq', 'tp')
- decode_out: bfloat16 [4, 5120], P(None, 'tp')
- log_probs: float32 [68, 152064], P(None, ('seq', 'tp'))
The draws below stay inside these ranges and needn't reach their ends.
Inputs may be any that keep to these rules, and one draw needn't show every extreme that they name: `prefix_lengths`: some request has no cached prefix and some has exactly 768 cached tokens. `cache_lengths`: some request has exactly 8192 cached tokens. `slot_table`: distinct slots.
All inputs are finite; a program needn't handle non-finite values.
Results may differ from the reference program's by a relative error of at most 0.0035.
Values may be sent and summed in bfloat16 or wider, within the bound.
A program may use at most 128 MiB of HBM per device.

```python
import math
import jax
import jax.numpy as jnp
from jax import lax

D = 5120
QUERY_HEADS = 40
KEY_HEADS = 8
HEAD_SIZE = 128
VOCAB = 152064
REQUEST_TOKENS = 128
PREFIX_POSITIONS = 768
DECODE_REQUESTS = 4
PREFILL_REQUESTS = 64
CACHE_SLOTS = 5
SLOT_POSITIONS = 8192
PREFILL_TOKENS = 8192


def bounded_gaussian(key, shape):
    return jax.random.truncated_normal(key, -4.0, 4.0, shape, jnp.float32)


def hidden_rows(key, entry_count):
    return bounded_gaussian(jax.random.fold_in(key, 1), (entry_count, D))


def repeat_heads(key_matrix, entry_count):
    deviation_scale = key_matrix.reshape(entry_count, KEY_HEADS, 1, HEAD_SIZE)
    return jnp.broadcast_to(deviation_scale, (entry_count, KEY_HEADS, QUERY_HEADS // KEY_HEADS, HEAD_SIZE)).reshape(entry_count, QUERY_HEADS * HEAD_SIZE)


def prefill_pair(key):
    random_seed_key = jax.random.fold_in(key, 700)
    sampled_values = bounded_gaussian(jax.random.fold_in(random_seed_key, 1), (2, PREFILL_TOKENS, KEY_HEADS * HEAD_SIZE))
    key_matrix = sampled_values[0]
    noise = bounded_gaussian(jax.random.fold_in(random_seed_key, 5), (PREFILL_TOKENS, QUERY_HEADS * HEAD_SIZE))
    query_matrix = noise
    return (jnp.stack([key_matrix, sampled_values[1]]), query_matrix)


def decode_set(key):
    random_seed_key = jax.random.fold_in(key, 800)
    sampled_values = bounded_gaussian(jax.random.fold_in(random_seed_key, 1), (2, DECODE_REQUESTS, KEY_HEADS * HEAD_SIZE))
    strength = jnp.full((DECODE_REQUESTS,), 0.5, jnp.float32)
    noise = bounded_gaussian(jax.random.fold_in(random_seed_key, 4), (DECODE_REQUESTS, QUERY_HEADS * HEAD_SIZE))
    query_matrix = noise + strength[:, None] * repeat_heads(sampled_values[0], DECODE_REQUESTS)
    return (sampled_values, query_matrix)


def slot_draw(key):
    random_seed_key = jax.random.fold_in(key, 300)
    order = jax.random.permutation(jax.random.fold_in(random_seed_key, 1), CACHE_SLOTS - 1)[:DECODE_REQUESTS - 1]
    table = jnp.concatenate([order.astype(jnp.int32), jnp.full((1,), CACHE_SLOTS - 1, jnp.int32)])
    return jax.random.permutation(jax.random.fold_in(random_seed_key, 2), table).astype(jnp.int32)


def draw_prefill_hidden(key, part):
    return hidden_rows(jax.random.fold_in(key, 601), PREFILL_TOKENS).astype(jnp.bfloat16)


def draw_decode_hidden(key, part):
    return hidden_rows(jax.random.fold_in(key, 602), DECODE_REQUESTS).astype(jnp.bfloat16)


def draw_prefill_query_rows(key, part):
    return prefill_pair(key)[1].astype(jnp.bfloat16)


def draw_prefill_key_value(key, part):
    return prefill_pair(key)[0].astype(jnp.bfloat16)


def draw_decode_query_rows(key, part):
    return decode_set(key)[1].astype(jnp.bfloat16)


def draw_decode_kv(key, part):
    return decode_set(key)[0].astype(jnp.bfloat16)


def draw_decode_slot_cache(key, part):
    slot_storage = bounded_gaussian(jax.random.fold_in(key, 900), (2, CACHE_SLOTS, SLOT_POSITIONS, KEY_HEADS * HEAD_SIZE))
    return slot_storage.astype(jnp.bfloat16)


def draw_slot_table(key, part):
    return slot_draw(key)


def draw_cache_lengths(key, part):
    random_seed_key = jax.random.fold_in(key, 400)
    sampled_values = jax.random.randint(jax.random.fold_in(random_seed_key, 1), (DECODE_REQUESTS,), SLOT_POSITIONS // 4, SLOT_POSITIONS + 1)
    chosen = jax.random.randint(jax.random.fold_in(random_seed_key, 2), (), 0, DECODE_REQUESTS)
    return jnp.where(jnp.arange(DECODE_REQUESTS) == chosen, SLOT_POSITIONS, sampled_values).astype(jnp.int32)


def draw_prefix_lengths(key, part):
    random_seed_key = jax.random.fold_in(key, 450)
    sampled_values = jax.random.randint(jax.random.fold_in(random_seed_key, 1), (PREFILL_REQUESTS,), 0, PREFIX_POSITIONS + 1)
    longest = jax.random.randint(jax.random.fold_in(random_seed_key, 2), (), 0, PREFILL_REQUESTS)
    empty_one = (longest + 1 + jax.random.randint(jax.random.fold_in(random_seed_key, 3), (), 0, PREFILL_REQUESTS - 1)) % PREFILL_REQUESTS
    place = jnp.arange(PREFILL_REQUESTS)
    sampled_values = jnp.where(place == longest, PREFIX_POSITIONS, sampled_values)
    return jnp.where(place == empty_one, 0, sampled_values).astype(jnp.int32)


def draw_head_weight(key, part):
    random_seed_key = jax.random.fold_in(key, 1000)
    column_place = jnp.arange(VOCAB).astype(jnp.float32) / VOCAB
    column_scale = 0.5 + 2.5 * column_place
    return (bounded_gaussian(jax.random.fold_in(random_seed_key, 1), (D, VOCAB)) / D ** 0.5 * column_scale[None, :]).astype(jnp.bfloat16)


def steps_of(stream_key, extent, cuts, smallest, high):
    level, own = 1.0, jax.random.fold_in(stream_key, 6)
    for position, parts in cuts:
        heights = jnp.exp(jax.random.uniform(jax.random.fold_in(own, position), (parts,), jnp.float32, smallest / len(cuts), high / len(cuts)))
        level = level * jnp.repeat(heights, extent[position] // parts).reshape([-1 if axis == position else 1 for axis in range(len(extent))])
    return level


def gaussian(rng, dims, scale, reach, shards=(), kind=jnp.bfloat16):
    level = steps_of(rng, dims, shards, -0.22, 0.18) if shards else 1.0
    values = jax.random.normal(rng, dims, jnp.float32) * scale * level
    return jnp.minimum(jnp.maximum(values, -reach), reach).astype(kind)


def setup_inputs(seed: int = 0) -> dict:
    streams_of = jax.random.split(jax.random.key(seed), 15)
    prefill_hidden = draw_prefill_hidden(jax.random.fold_in(streams_of[14], 71), 0)
    prefill_query_rows = draw_prefill_query_rows(jax.random.fold_in(streams_of[14], 71), 0)
    prefill_key_value = draw_prefill_key_value(jax.random.fold_in(streams_of[14], 71), 0)
    request_prefix_cache = gaussian(streams_of[3], (2, PREFILL_REQUESTS, PREFIX_POSITIONS, KEY_HEADS * HEAD_SIZE), 1.0, 5.0, ((1, 64), (3, 8)))
    prefix_lengths = draw_prefix_lengths(jax.random.fold_in(streams_of[14], 71), 0)
    decode_hidden = draw_decode_hidden(jax.random.fold_in(streams_of[14], 71), 0)
    decode_query_rows = draw_decode_query_rows(jax.random.fold_in(streams_of[14], 71), 0)
    decode_kv = draw_decode_kv(jax.random.fold_in(streams_of[14], 71), 0)
    decode_slot_cache = draw_decode_slot_cache(jax.random.fold_in(streams_of[14], 71), 0)
    cache_lengths = draw_cache_lengths(jax.random.fold_in(streams_of[14], 71), 0)
    slot_table = draw_slot_table(jax.random.fold_in(streams_of[14], 71), 0)
    out_weight = gaussian(streams_of[11], (QUERY_HEADS * HEAD_SIZE, D), (QUERY_HEADS * HEAD_SIZE) ** -0.5, 0.078125, ((0, 8), (1, 64)))
    final_gain = jnp.clip(1.0 + 0.1 * jax.random.normal(streams_of[12], (D,), jnp.float32), 0.5, 1.5).astype(jnp.bfloat16)
    head_weight = draw_head_weight(jax.random.fold_in(streams_of[14], 71), 0)
    return {"prefill_hidden": prefill_hidden, "prefill_query_rows": prefill_query_rows, "prefill_key_value": prefill_key_value, "request_prefix_cache": request_prefix_cache, "prefix_lengths": prefix_lengths, "decode_hidden": decode_hidden, "decode_query_rows": decode_query_rows, "decode_kv": decode_kv, "decode_slot_cache": decode_slot_cache, "cache_lengths": cache_lengths, "slot_table": slot_table, "out_weight": out_weight, "final_gain": final_gain, "head_weight": head_weight}


neg_large = -1e+30
exact = lax.Precision.HIGHEST
norm_eps = 1e-06

def reference(prefill_hidden, prefill_query_rows, prefill_key_value, request_prefix_cache, prefix_lengths, decode_hidden, decode_query_rows, decode_kv, decode_slot_cache, cache_lengths, slot_table, out_weight, final_gain, head_weight):
    query_group_width = QUERY_HEADS // KEY_HEADS
    score_scale = 1.0 / math.sqrt(HEAD_SIZE)
    query_matrix = prefill_query_rows.reshape(PREFILL_REQUESTS, REQUEST_TOKENS, KEY_HEADS, query_group_width, HEAD_SIZE)
    request_key_value = jnp.transpose(prefill_key_value.reshape(2, PREFILL_REQUESTS, REQUEST_TOKENS, KEY_HEADS * HEAD_SIZE), (1, 0, 2, 3))
    prefix_all = jnp.transpose(request_prefix_cache, (1, 0, 2, 3))

    def prefill_one(inputs):
        query_rows, prefix_token_rows, current_rows, prefix_end = inputs
        joined_keys = jnp.concatenate([prefix_token_rows[0], current_rows[0]], 0).reshape(PREFIX_POSITIONS + REQUEST_TOKENS, KEY_HEADS, HEAD_SIZE).astype(jnp.float32)
        value_matrix = jnp.concatenate([prefix_token_rows[1], current_rows[1]], 0).reshape(PREFIX_POSITIONS + REQUEST_TOKENS, KEY_HEADS, HEAD_SIZE).astype(jnp.float32)
        key_place = jnp.arange(PREFIX_POSITIONS + REQUEST_TOKENS)
        query_place = jnp.arange(REQUEST_TOKENS)
        live_mask = jnp.where(key_place[None, :] < PREFIX_POSITIONS, key_place[None, :] < prefix_end, key_place[None, :] - PREFIX_POSITIONS <= query_place[:, None])
        scores = jnp.einsum('rkgh,skh->kgrs', query_rows.astype(jnp.float32), joined_keys, precision=exact) * score_scale
        masked = jnp.where(live_mask, scores, neg_large)
        row_max = lax.optimization_barrier(jnp.max(masked, axis=-1, keepdims=True))
        weights = jnp.where(live_mask, jnp.exp(masked - row_max), 0.0)
        row_sum = lax.optimization_barrier(jnp.sum(weights, axis=-1))
        weights_low = weights.astype(jnp.bfloat16).astype(jnp.float32)
        mixed = jnp.einsum('kgrs,skh->rkgh', weights_low, value_matrix, precision=exact)
        result = mixed / jnp.transpose(row_sum, (2, 0, 1))[..., None]
        return result.astype(jnp.bfloat16).reshape(REQUEST_TOKENS, QUERY_HEADS * HEAD_SIZE)
    prefill_attention = lax.map(prefill_one, (query_matrix, prefix_all, request_key_value, prefix_lengths)).reshape(PREFILL_TOKENS, QUERY_HEADS * HEAD_SIZE)
    decode_token_rows = decode_query_rows.reshape(DECODE_REQUESTS, KEY_HEADS, query_group_width, HEAD_SIZE)
    fresh_all = jnp.transpose(decode_kv, (1, 0, 2))

    def decode_one(inputs):
        query_rows, cache_slot_index, cache_len, current_rows = inputs
        joined_keys = jnp.concatenate([decode_slot_cache[0, cache_slot_index], current_rows[0][None]], 0).reshape(SLOT_POSITIONS + 1, KEY_HEADS, HEAD_SIZE).astype(jnp.float32)
        value_matrix = jnp.concatenate([decode_slot_cache[1, cache_slot_index], current_rows[1][None]], 0).reshape(SLOT_POSITIONS + 1, KEY_HEADS, HEAD_SIZE).astype(jnp.float32)
        key_place = jnp.arange(SLOT_POSITIONS + 1)
        live_mask = (key_place < cache_len) | (key_place == SLOT_POSITIONS)
        scores = jnp.einsum('kgh,skh->kgs', query_rows.astype(jnp.float32), joined_keys, precision=exact) * score_scale
        masked = jnp.where(live_mask, scores, neg_large)
        row_max = lax.optimization_barrier(jnp.max(masked, axis=-1, keepdims=True))
        weights = jnp.where(live_mask, jnp.exp(masked - row_max), 0.0)
        row_sum = lax.optimization_barrier(jnp.sum(weights, axis=-1))
        mixed = jnp.einsum('kgs,skh->kgh', weights, value_matrix, precision=exact)
        return (mixed / row_sum[..., None]).astype(jnp.bfloat16).reshape(QUERY_HEADS * HEAD_SIZE)
    decode_attention = lax.map(decode_one, (decode_token_rows, slot_table, cache_lengths, fresh_all))
    attention_all = jnp.concatenate([prefill_attention, decode_attention], 0)
    projected = jnp.dot(attention_all, out_weight, preferred_element_type=jnp.float32)
    residual = jnp.concatenate([prefill_hidden, decode_hidden], 0).astype(jnp.float32)
    updated = (residual + projected).astype(jnp.bfloat16)
    prefill_out = updated[:PREFILL_TOKENS]
    decode_out = updated[PREFILL_TOKENS:]
    head_input = jnp.concatenate([decode_out, prefill_out[REQUEST_TOKENS - 1::REQUEST_TOKENS]], 0).astype(jnp.float32)
    mean_square = lax.optimization_barrier(jnp.mean(head_input * head_input, axis=-1, keepdims=True))
    normed = (head_input * lax.rsqrt(mean_square + norm_eps) * final_gain.astype(jnp.float32)).astype(jnp.bfloat16)
    logits = jnp.dot(normed, head_weight, preferred_element_type=jnp.float32)
    row_max = lax.optimization_barrier(jnp.max(logits, axis=-1, keepdims=True))
    row_sum = lax.optimization_barrier(jnp.sum(jnp.exp(logits - row_max), axis=-1, keepdims=True))
    log_probs = logits - (row_max + jnp.log(row_sum))
    return (prefill_out, decode_out, log_probs)
```

```python
import math

import jax
import jax.numpy as jnp
from jax import lax
from jax.experimental import pallas as pl
from jax.experimental.pallas import tpu as pltpu
from jax.sharding import PartitionSpec as P

NEG = -1e30
EPS = 1e-6
NT = (((1,), (1,)), ((), ()))
MESH = pl.DeviceIdType.MESH
F32 = jnp.float32
BF16 = jnp.bfloat16

NX, NY, NZ, NC = 4, 4, 16, 2
WC = 80
HD = 128
GROUP = 5
KW = 640


def fori(lo, hi, body):
    def step(i, carry):
        body(i)
        return carry

    lax.fori_loop(lo, hi, step, 0)


def mod(a, n):
    return lax.rem(a + n, n)


def kernel(
    prefix_len_ref,
    cache_len_ref,
    slot_ref,
    hid_ref,
    q_ref,
    kv_ref,
    pre_ref,
    dhid_ref,
    dq_ref,
    dkv_ref,
    dcache_ref,
    w_ref,
    gain_ref,
    hw_ref,
    out_ref,
    dout_ref,
    lp_ref,
    hwbuf,
    wbuf,
    abuf,
    qd,
    dpart,
    dxb,
    dz1,
    dz2,
    dfin,
    dmat,
    cs_main,
    cs_dec,
    cr_main,
    cr_dec,
    co_main,
    co_dec,
    msg,
    rbuf,
    big,
    agz,
    hbuf,
    tmat,
    lst,
    lsz,
    hw_sem,
    wr_s,
    wr_r,
    wl_s,
    wl_r,
    a_s,
    a_r,
    dx_s,
    dx_r,
    d1_s,
    d1_r,
    d2_s,
    d2_r,
    df_s,
    df_r,
    cm_s,
    cm_r,
    cd_s,
    cd_r,
    r_s,
    r_r,
    gz_s,
    gz_r,
    hb_s,
    hb_r,
    hc_s,
    hc_r,
    db_s,
    db_r,
    dc_s,
    dc_r,
    ls_s,
    ls_r,
    lz_s,
    lz_r,
):
    s = lax.axis_index("seq")
    t = lax.axis_index("tp")
    z, x = lax.div(s, NX), lax.rem(s, NX)
    y, c = lax.div(t, NC), lax.rem(t, NC)
    scale = 1.0 / math.sqrt(HD)

    def dev(zz, xx, yy, cc):
        return (zz * NX + xx, yy * NC + cc)

    def rcopy(src, dst, ss, rs, device):
        return pltpu.make_async_remote_copy(
            src_ref=src, dst_ref=dst, send_sem=ss, recv_sem=rs, device_id=device, device_id_type=MESH
        )

    hw_copy = pltpu.make_async_copy(hw_ref, hwbuf, hw_sem)
    hw_copy.start()

    barrier = pltpu.get_barrier_semaphore()

    def plane(p):
        q = lax.rem(x * 8 + t + p, 32)
        return (z * NX + lax.div(q, 8), lax.rem(q, 8))

    def sig_z(d):
        pl.semaphore_signal(barrier, inc=1, device_id=dev(mod(z + d, NZ), x, y, c), device_id_type=MESH)

    def sig_p(p):
        pl.semaphore_signal(barrier, inc=1, device_id=plane(p), device_id_type=MESH)

    fori(1, NZ, sig_z)
    fori(1, 32, sig_p)

    eye = (
        lax.broadcasted_iota(jnp.int32, (WC, WC), 0) == lax.broadcasted_iota(jnp.int32, (WC, WC), 1)
    ).astype(F32).astype(BF16)
    wbuf[z] = lax.dot_general(eye, w_ref[...], NT, preferred_element_type=F32).astype(BF16)

    qd[...] = jnp.zeros_like(qd)
    dq = dq_ref[...].astype(F32)
    for r in range(4):
        for h in range(GROUP):
            qd[r * 8 + h : r * 8 + h + 1, :] = dq[r : r + 1, h * HD : (h + 1) * HD]
    qall = qd[...].astype(BF16)
    row = lax.broadcasted_iota(jnp.int32, (32, 1), 0)
    rows_slot = jnp.zeros((32, 1), jnp.int32)
    rows_len = jnp.zeros((32, 1), jnp.int32)
    for r in range(4):
        inside = lax.div(row, 8) == r
        rows_slot = jnp.where(inside, slot_ref[r], rows_slot)
        rows_len = jnp.where(inside, cache_len_ref[r], rows_len)
    keys = dcache_ref[0].reshape(5 * 128, HD)
    vals = dcache_ref[1].reshape(5 * 128, HD)
    col = lax.broadcasted_iota(jnp.int32, (32, 640), 1)
    live = (lax.div(col, 128) == rows_slot) & (s * 128 + lax.rem(col, 128) < rows_len)
    sc = lax.dot_general(qall, keys, NT, preferred_element_type=F32) * scale
    sc = jnp.where(live, sc, NEG)
    dm = jnp.max(sc, axis=-1, keepdims=True)
    dw = jnp.where(live, jnp.exp(sc - dm), 0.0)
    dl = jnp.sum(dw, axis=-1, keepdims=True)
    hi = dw.astype(BF16)
    lo = (dw - hi.astype(F32)).astype(BF16)
    do = jnp.dot(hi, vals, preferred_element_type=F32) + jnp.dot(lo, vals, preferred_element_type=F32)
    lane = lax.broadcasted_iota(jnp.int32, (32, HD), 1)
    dstat = jnp.where(lane < 64, dm, dl)
    for r in range(4):
        dpart[r, 0:8, :] = do[r * 8 : r * 8 + 8]
        dpart[r, 8:16, :] = dstat[r * 8 : r * 8 + 8]

    pl.semaphore_wait(barrier, NZ - 1 + 31)

    def w_right(k):
        b = mod(z - k + 1, NZ)
        return rcopy(wbuf.at[b], wbuf.at[b], wr_s.at[k], wr_r.at[k], dev(mod(z + 1, NZ), x, y, c))

    def w_left(k):
        b = mod(z + k - 1, NZ)
        return rcopy(wbuf.at[b], wbuf.at[b], wl_s.at[k], wl_r.at[k], dev(mod(z - 1, NZ), x, y, c))

    def w_right_in(k):
        b = mod(z - k, NZ)
        return rcopy(wbuf.at[b], wbuf.at[b], wr_s.at[k], wr_r.at[k], dev(mod(z + 1, NZ), x, y, c))

    def w_left_in(k):
        b = mod(z + k, NZ)
        return rcopy(wbuf.at[b], wbuf.at[b], wl_s.at[k], wl_r.at[k], dev(mod(z - 1, NZ), x, y, c))

    def w_forward(k):
        w_right_in(k).wait_recv()
        if k < 8:
            w_right(k + 1).start()
        if k < 8:
            w_left_in(k).wait_recv()
            if k < 7:
                w_left(k + 1).start()

    w_right(1).start()
    w_left(1).start()

    def dx(d):
        xx = mod(x + d, NX)
        return rcopy(dpart.at[xx], dxb.at[x], dx_s.at[d], dx_r.at[d], dev(z, xx, y, c))

    dxb[x] = dpart[x]
    fori(1, NX, lambda d: dx(d).start())

    pe = prefix_len_ref[s]
    kp, ko = pre_ref[0, 0], kv_ref[0]
    vp, vo = pre_ref[1, 0], kv_ref[1]
    n_pre = kp.shape[0]
    live1 = lax.broadcasted_iota(jnp.int32, (128, n_pre), 1) < pe
    live2 = lax.broadcasted_iota(jnp.int32, (128, 128), 1) <= lax.broadcasted_iota(jnp.int32, (128, 128), 0)

    def head(h):
        hs = pl.ds(pl.multiple_of(h * HD, HD), HD)
        qh = q_ref[:, hs]
        s1 = lax.dot_general(qh, kp, NT, preferred_element_type=F32) * scale
        s2 = lax.dot_general(qh, ko, NT, preferred_element_type=F32) * scale
        s1 = jnp.where(live1, s1, NEG)
        s2 = jnp.where(live2, s2, NEG)
        m = jnp.maximum(jnp.max(s1, -1, keepdims=True), jnp.max(s2, -1, keepdims=True))
        p1 = jnp.where(live1, jnp.exp(s1 - m), 0.0)
        p2 = jnp.where(live2, jnp.exp(s2 - m), 0.0)
        total = jnp.sum(p1, -1, keepdims=True) + jnp.sum(p2, -1, keepdims=True)
        o = jnp.dot(p1.astype(BF16), vp, preferred_element_type=F32)
        o += jnp.dot(p2.astype(BF16), vo, preferred_element_type=F32)
        abuf[x, :, hs] = (o / total).astype(BF16)

    fori(0, GROUP, head)
    w_forward(1)

    def a_copy(d, src):
        return rcopy(abuf.at[src], abuf.at[src], a_s.at[d], a_r.at[d], dev(z, mod(x + d, NX), y, c))

    fori(1, NX, lambda d: a_copy(d, x).start())

    def merge(ref):
        os = [ref[i, 0:8, :] for i in range(4)]
        st = [ref[i, 8:16, :] for i in range(4)]
        ms = [a[:, 0:1] for a in st]
        lls = [a[:, 64:65] for a in st]
        m = jnp.maximum(jnp.maximum(ms[0], ms[1]), jnp.maximum(ms[2], ms[3]))
        o, l = 0.0, 0.0
        for i in range(4):
            f = jnp.exp(ms[i] - m)
            o = o + os[i] * f
            l = l + lls[i] * f
        return o, m, l

    lane8 = lax.broadcasted_iota(jnp.int32, (8, HD), 1)

    def dx_in(d):
        return rcopy(dpart.at[x], dxb.at[mod(x - d, NX)], dx_s.at[d], dx_r.at[d], dev(z, mod(x + d, NX), y, c))

    fori(1, NX, lambda d: dx_in(d).wait_recv())
    o, m, l = merge(dxb)
    zl, zg = lax.rem(z, 4), lax.div(z, 4)
    dz1[zl, 0:8, :] = o
    dz1[zl, 8:16, :] = jnp.where(lane8 < 64, m, l)

    def d1(d, slot):
        return rcopy(dz1.at[slot], dz1.at[slot], d1_s.at[d], d1_r.at[d], dev(zg * 4 + mod(zl + d, 4), x, y, c))

    fori(1, 4, lambda d: d1(d, zl).start())
    w_forward(2)
    fori(1, 4, lambda d: d1(d, mod(zl - d, 4)).wait_recv())
    o, m, l = merge(dz1)
    dz2[zg, 0:8, :] = o
    dz2[zg, 8:16, :] = jnp.where(lane8 < 64, m, l)

    def d2(d, slot):
        return rcopy(dz2.at[slot], dz2.at[slot], d2_s.at[d], d2_r.at[d], dev(mod(zg + d, 4) * 4 + zl, x, y, c))

    fori(1, 4, lambda d: d2(d, zg).start())
    w_forward(3)
    fori(1, 4, lambda d: d2(d, mod(zg - d, 4)).wait_recv())
    o, m, l = merge(dz2)
    row4 = lax.broadcasted_iota(jnp.int32, (4, HD), 0)
    own_k = jnp.sum(jnp.where(row4 == x, dkv_ref[0].astype(F32), 0.0), axis=0, keepdims=True)
    own_v = jnp.sum(jnp.where(row4 == x, dkv_ref[1].astype(F32), 0.0), axis=0, keepdims=True)
    own_q = qd[pl.ds(pl.multiple_of(x * 8, 8), 8), :]
    own_s = jnp.sum(own_q * own_k, axis=-1, keepdims=True) * scale
    m2 = jnp.maximum(m, own_s)
    f1, f2 = jnp.exp(m - m2), jnp.exp(own_s - m2)
    dfin[x] = (o * f1 + own_v * f2) / (l * f1 + f2)

    def df(d, slot):
        return rcopy(dfin.at[slot], dfin.at[slot], df_s.at[d], df_r.at[d], dev(z, mod(x + d, NX), y, c))

    fori(1, NX, lambda d: df(d, x).start())
    w_forward(4)
    fori(1, NX, lambda d: df(d, mod(x - d, NX)).wait_recv())
    dmat[...] = jnp.zeros_like(dmat)
    for r in range(4):
        for h in range(GROUP):
            dmat[r : r + 1, h * HD : (h + 1) * HD] = dfin[r, h : h + 1, :]
    w_forward(5)
    fori(1, NX, lambda d: a_copy(d, mod(x - d, NX)).wait_recv())
    w_forward(6)
    w_forward(7)
    w_forward(8)

    cs_dec[...] = jnp.zeros_like(cs_dec)
    co_dec[...] = jnp.zeros_like(co_dec)

    def product(g, cc, main, dec):
        a = abuf[...].reshape(4 * 128, KW)
        db = dmat[...].astype(BF16)
        for j in range(2):
            wt = wbuf[g * 4 + cc * 2 + j]
            main[j * WC : (j + 1) * WC, :] = lax.dot_general(wt, a, NT, preferred_element_type=F32)
            dd = lax.dot_general(db, wt, NT, preferred_element_type=F32)
            dec[j * 8 : j * 8 + 8, 0:WC] = dd[0:8]

    def cm(d):
        return rcopy(cs_main.at[d], cr_main.at[d], cm_s.at[d], cm_r.at[d], dev(z, x, y, 1 - c))

    def cd(d):
        return rcopy(cs_dec.at[d], cr_dec.at[d], cd_s.at[d], cd_r.at[d], dev(z, x, y, 1 - c))

    def make(d):
        g = mod(y + d, NY)
        product(g, 1 - c, cs_main.at[d], cs_dec.at[d])
        cm(d).start()
        cd(d).start()
        product(g, c, co_main.at[d], co_dec.at[d])

    def r_copy(d, xx):
        return rcopy(
            msg.at[d * 4 + xx],
            rbuf.at[x * 4 + y],
            r_s.at[d * 4 + xx],
            r_r.at[x * 4 + y],
            dev(z, xx, mod(y + d, NY), c),
        )

    def finish(d):
        cm(d).wait_recv()
        cd(d).wait_recv()
        dec = (co_dec[d] + cr_dec[d]).astype(BF16)
        for xx in range(NX):
            ls = slice(xx * 128, (xx + 1) * 128)
            msg[d * 4 + xx, 0:160, :] = (co_main[d, :, ls] + cr_main[d, :, ls]).astype(BF16)
            msg[d * 4 + xx, 160:176, :] = dec

        def go(xx):
            @pl.when((d != 0) | (xx != x))
            def _():
                r_copy(d, xx).start()

        fori(0, NX, go)

    def steps(i):
        @pl.when(i < 4)
        def _():
            make(lax.rem(i + 1, NY))

        @pl.when(i > 0)
        def _():
            finish(lax.rem(i, NY))

    fori(0, 5, steps)
    rbuf[x * 4 + y] = msg[x]

    def r_in(p):
        src = lax.rem(x * 4 + y + p, 16)
        return rcopy(msg.at[0], rbuf.at[src], r_s.at[0], r_r.at[src], dev(z, x, y, 1 - c))

    fori(1, 16, lambda p: r_in(p).wait_recv())

    dlane = lax.broadcasted_iota(jnp.int32, (8, HD), 1)
    dproj = jnp.zeros((8, KW), F32)
    for xs in range(NX):
        tot = rbuf[xs * 4].astype(F32)
        for ys in range(1, NY):
            tot += rbuf[xs * 4 + ys].astype(F32)
        for j in range(2):
            blk = j * 4 + xs
            big[blk * WC : (blk + 1) * WC, :] = tot[j * WC : (j + 1) * WC, :]
            piece = jnp.where(dlane < WC, tot[160 + j * 8 : 168 + j * 8, :], 0.0)
            wide = jnp.concatenate([piece, jnp.zeros((8, KW - HD), F32)], axis=1)
            dproj += pltpu.roll(wide, blk * WC, 1) if blk else wide
    dres = (dhid_ref[...].astype(F32) + dproj[0:4]).astype(BF16)
    dout_ref[...] = dres
    agz[z] = jnp.zeros((8, HD), F32)
    for h in range(GROUP):
        ls = slice(h * HD, (h + 1) * HD)
        res = (hid_ref[:, ls].astype(F32) + big[ls, :].T).astype(BF16)
        out_ref[:, ls] = res
        agz[z, h : h + 1, :] = res.astype(F32)[127:128, :]

    def gz(d, slot):
        return rcopy(agz.at[slot], agz.at[slot], gz_s.at[d], gz_r.at[d], dev(mod(z + d, NZ), x, y, c))

    fori(1, NZ, lambda d: gz(d, z).start())

    def drows(tt):
        return hbuf.at[pl.ds(64, 16), pl.ds(pl.multiple_of(tt * KW, HD), KW)]

    def hrows(xx, tt):
        return hbuf.at[pl.ds(pl.multiple_of(xx * 16, 16), 16), pl.ds(pl.multiple_of(tt * KW, HD), KW)]

    drows(t)[...] = jnp.concatenate([dres.astype(F32), jnp.zeros((12, KW), F32)], axis=0).astype(BF16)

    def dbc(d, yy):
        ref = drows(yy * NC + c)
        return rcopy(ref, ref, db_s.at[d], db_r.at[d], dev(z, x, mod(y + d, NY), c))

    def dcc(d, yy, cc):
        ref = drows(yy * NC + cc)
        return rcopy(ref, ref, dc_s.at[d], dc_r.at[d], dev(z, x, y, 1 - c))

    fori(1, NY, lambda d: dbc(d, y).start())
    dcc(0, y, c).start()

    def dfwd(d):
        yy = mod(y - d, NY)
        dbc(d, yy).wait_recv()
        dcc(d, yy, c).start()

    fori(1, NZ, lambda d: gz(d, mod(z - d, NZ)).wait_recv())
    flat = agz.reshape(NZ * 8, HD)
    for h in range(GROUP):
        rows = flat[pl.ds(h, NZ, stride=8), :].astype(BF16)
        hbuf[pl.ds(pl.multiple_of(x * 16, 16), 16), pl.ds(pl.multiple_of(t * KW + h * HD, HD), HD)] = rows

    def hbc(p, i):
        q = lax.rem(x * 4 + y + p, 16)
        ref = hrows(lax.div(i, 4), lax.rem(i, 4) * NC + c)
        return rcopy(ref, ref, hb_s.at[p], hb_r.at[p], dev(z, lax.div(q, 4), lax.rem(q, 4), c))

    def hcc(p, i, cc):
        ref = hrows(lax.div(i, 4), lax.rem(i, 4) * NC + cc)
        return rcopy(ref, ref, hc_s.at[p], hc_r.at[p], dev(z, x, y, 1 - c))

    fori(1, 16, lambda p: hbc(p, x * 4 + y).start())
    hcc(0, x * 4 + y, c).start()
    fori(1, NY, dfwd)

    def hfwd(p):
        i = lax.rem(x * 4 + y - p + 16, 16)
        hbc(p, i).wait_recv()
        hcc(p, i, c).start()

    fori(1, 16, hfwd)
    fori(0, NY, lambda d: dcc(d, mod(y - d, NY), 1 - c).wait_recv())
    fori(0, 16, lambda p: hcc(p, lax.rem(x * 4 + y - p + 16, 16), 1 - c).wait_recv())
    hw_copy.wait()

    def chunk(i):
        return pl.ds(pl.multiple_of(i * KW, HD), KW)

    def square(i, acc):
        v = hbuf[:, chunk(i)].astype(F32)
        return acc + jnp.sum(v * v, axis=-1, keepdims=True)

    ssq = lax.fori_loop(0, 8, square, jnp.zeros((80, 1), F32))
    inv = lax.rsqrt(ssq / 5120.0 + EPS)
    vocab = hwbuf.shape[1]

    def logit(i, acc):
        v = hbuf[:, chunk(i)].astype(F32)
        n = (v * inv * gain_ref[:, chunk(i)].astype(F32)).astype(BF16)
        return acc + jnp.dot(
            n, hwbuf[pl.ds(pl.multiple_of(i * KW, HD), KW), :], preferred_element_type=F32
        )

    logits = lax.fori_loop(0, 8, logit, jnp.zeros((80, vocab), F32))
    lm = jnp.max(logits, axis=-1, keepdims=True)
    ll = jnp.sum(jnp.exp(logits - lm), axis=-1, keepdims=True)

    ln = lax.broadcasted_iota(jnp.int32, (80, HD), 1)
    tmat[...] = jnp.zeros_like(tmat)
    tmat[0:80, :] = jnp.where(ln == 0, lm, jnp.where(ln == 1, ll, 0.0))
    me = x * 8 + t
    lst[me] = tmat[...].T[0:8, :]

    def lsc(p, i):
        return rcopy(lst.at[i], lst.at[i], ls_s.at[p], ls_r.at[p], plane(p))

    fori(1, 32, lambda p: lsc(p, me).start())
    fori(1, 32, lambda p: lsc(p, lax.rem(me - p + 32, 32)).wait_recv())

    def join(ref, n):
        f = ref.reshape(n * 8, HD)
        ms = f[pl.ds(0, n, stride=8), :]
        lls = f[pl.ds(1, n, stride=8), :]
        top = jnp.max(ms, axis=0, keepdims=True)
        return top, jnp.sum(lls * jnp.exp(ms - top), axis=0, keepdims=True)

    top, tot = join(lst, 32)
    r8 = lax.broadcasted_iota(jnp.int32, (8, HD), 0)
    lsz[z] = jnp.where(r8 == 0, top, tot)

    def lzc(d, i):
        return rcopy(lsz.at[i], lsz.at[i], lz_s.at[d], lz_r.at[d], dev(mod(z + d, NZ), x, y, c))

    fori(1, NZ, lambda d: lzc(d, z).start())
    fori(1, NZ, lambda d: lzc(d, mod(z - d, NZ)).wait_recv())
    top, tot = join(lsz, NZ)
    tmat[...] = jnp.broadcast_to(top + jnp.log(tot), (HD, HD))
    lse = tmat[...].T[0:80, 0:1]
    lp = logits - lse
    lp_ref[0:4, :] = lp[64:68]
    for i in range(64):
        xx, zz = i // 16, i % 16
        lp_ref[4 + zz * 4 + xx : 5 + zz * 4 + xx, :] = lp[i : i + 1]

    for k in range(1, 9):
        w_right(k).wait_send()
    for k in range(1, 8):
        w_left(k).wait_send()

    def three(d):
        dx(d).wait_send()
        a_copy(d, x).wait_send()
        d1(d, zl).wait_send()
        d2(d, zg).wait_send()
        df(d, x).wait_send()
        dbc(d, y).wait_send()

    fori(1, 4, three)

    def four(d):
        cm(d).wait_send()
        cd(d).wait_send()
        dcc(d, mod(y - d, NY), c).wait_send()

        def one(xx):
            @pl.when((d != 0) | (xx != x))
            def _():
                r_copy(d, xx).wait_send()

        fori(0, NX, one)

    fori(0, 4, four)

    def fifteen(d):
        gz(d, z).wait_send()
        hbc(d, x * 4 + y).wait_send()
        lzc(d, z).wait_send()

    fori(1, 16, fifteen)
    fori(0, 16, lambda p: hcc(p, lax.rem(x * 4 + y - p + 16, 16), c).wait_send())
    fori(1, 32, lambda p: lsc(p, me).wait_send())


def local(
    prefill_hidden,
    prefill_query_rows,
    prefill_key_value,
    request_prefix_cache,
    prefix_lengths,
    decode_hidden,
    decode_query_rows,
    decode_kv,
    decode_slot_cache,
    cache_lengths,
    slot_table,
    out_weight,
    final_gain,
    head_weight,
):
    vocab = head_weight.shape[1]
    vm = pl.BlockSpec(memory_space=pltpu.VMEM)
    sm = pl.BlockSpec(memory_space=pltpu.SMEM)
    dma = lambda n: pltpu.SemaphoreType.DMA((n,))
    sems = []
    for n in (9, 8, 4, 4, 4, 4, 4, 4, 4, 16, 16, 16, 16, 4, 4, 32, 16):
        sems += [dma(n), dma(n)]
    return pl.pallas_call(
        kernel,
        out_shape=(
            jax.ShapeDtypeStruct((128, KW), BF16),
            jax.ShapeDtypeStruct((4, KW), BF16),
            jax.ShapeDtypeStruct((68, vocab), F32),
        ),
        in_specs=[sm, sm, sm] + [vm] * 10 + [pl.BlockSpec(memory_space=pl.ANY)],
        out_specs=(vm, vm, vm),
        scratch_shapes=[
            pltpu.VMEM(head_weight.shape, BF16),
            pltpu.VMEM((NZ, WC, KW), BF16),
            pltpu.VMEM((NX, 128, KW), BF16),
            pltpu.VMEM((32, HD), F32),
            pltpu.VMEM((4, 16, HD), F32),
            pltpu.VMEM((4, 16, HD), F32),
            pltpu.VMEM((4, 16, HD), F32),
            pltpu.VMEM((4, 16, HD), F32),
            pltpu.VMEM((4, 8, HD), F32),
            pltpu.VMEM((16, KW), F32),
            pltpu.VMEM((4, 160, 512), F32),
            pltpu.VMEM((4, 16, HD), F32),
            pltpu.VMEM((4, 160, 512), F32),
            pltpu.VMEM((4, 16, HD), F32),
            pltpu.VMEM((4, 160, 512), F32),
            pltpu.VMEM((4, 16, HD), F32),
            pltpu.VMEM((16, 176, HD), BF16),
            pltpu.VMEM((16, 176, HD), BF16),
            pltpu.VMEM((KW, HD), F32),
            pltpu.VMEM((NZ, 8, HD), F32),
            pltpu.VMEM((80, 5120), BF16),
            pltpu.VMEM((HD, HD), F32),
            pltpu.VMEM((32, 8, HD), F32),
            pltpu.VMEM((NZ, 8, HD), F32),
            pltpu.SemaphoreType.DMA,
            *sems,
        ],
        compiler_params=pltpu.CompilerParams(
            collective_id=0, has_side_effects=True, vmem_limit_bytes=48 * 1024 * 1024
        ),
    )(
        prefix_lengths,
        cache_lengths,
        slot_table,
        prefill_hidden,
        prefill_query_rows,
        prefill_key_value,
        request_prefix_cache,
        decode_hidden,
        decode_query_rows,
        decode_kv,
        decode_slot_cache,
        out_weight,
        final_gain.reshape(1, -1),
        head_weight,
    )


def solution(mesh):
    return jax.shard_map(
        local,
        mesh=mesh,
        in_specs=(
            P("seq", "tp"),
            P("seq", "tp"),
            P(None, "seq", "tp"),
            P(None, "seq", None, "tp"),
            P(),
            P(None, "tp"),
            P(None, "tp"),
            P(None, None, "tp"),
            P(None, None, "seq", "tp"),
            P(),
            P(),
            P("tp", "seq"),
            P(),
            P(None, ("seq", "tp")),
        ),
        out_specs=(P("seq", "tp"), P(None, "tp"), P(None, ("seq", "tp"))),
        check_vma=False,
    )
```

```python
import math

import jax
import jax.numpy as jnp
from jax import lax
from jax.experimental import pallas as pl
from jax.experimental.pallas import tpu as pltpu
from jax.sharding import PartitionSpec as P

NEG = -1e30
EPS = 1e-6
NT = (((1,), (1,)), ((), ()))
MESH = pl.DeviceIdType.MESH
F32 = jnp.float32
BF16 = jnp.bfloat16

NX, NY, NZ, NC = 4, 4, 16, 2
NCH = 5
WR = 16
WC = 80
HD = 128
GROUP = 5
KW = 640


def fori(lo, hi, body):
    def step(i, carry):
        body(i)
        return carry

    lax.fori_loop(lo, hi, step, 0)


def mod(a, n):
    return lax.rem(a + n, n)


def kernel(
    prefix_len_ref,
    cache_len_ref,
    slot_ref,
    hid_ref,
    q_ref,
    kv_ref,
    pre_ref,
    dhid_ref,
    dq_ref,
    dkv_ref,
    dcache_ref,
    w_ref,
    gain_ref,
    hw_ref,
    out_ref,
    dout_ref,
    lp_ref,
    hwbuf,
    wbuf,
    abuf,
    qd,
    dpart,
    dxb,
    dz1,
    dz2,
    dfin,
    dmat,
    dtmp,
    lrow,
    rows,
    hres,
    hs_buf,
    hr_buf,
    ho_buf,
    hmsg,
    hrb,
    cs_main,
    cr_main,
    co_main,
    msg,
    rbuf,
    big,
    agz,
    hbuf,
    tmat,
    lst,
    lsz,
    qv,
    prev,
    dcv,
    hw_sem,
    in_sem,
    wr_s,
    wr_r,
    wl_s,
    wl_r,
    a_s,
    a_r,
    dx_s,
    dx_r,
    d1_s,
    d1_r,
    d2_s,
    d2_r,
    df_s,
    df_r,
    lx_s,
    lx_r,
    hx_s,
    hx_r,
    hm_s,
    hm_r,
    cm_s,
    cm_r,
    r_s,
    r_r,
    gz_s,
    gz_r,
    hb_s,
    hb_r,
    hc_s,
    hc_r,
    db_s,
    db_r,
    dc_s,
    dc_r,
    ls_s,
    ls_r,
    lz_s,
    lz_r,
):
    s = lax.axis_index("seq")
    t = lax.axis_index("tp")
    z, x = lax.div(s, NX), lax.rem(s, NX)
    y, c = lax.div(t, NC), lax.rem(t, NC)
    scale = 1.0 / math.sqrt(HD)

    def dev(zz, xx, yy, cc):
        return (zz * NX + xx, yy * NC + cc)

    def rcopy(src, dst, ss, rs, device):
        return pltpu.make_async_remote_copy(
            src_ref=src, dst_ref=dst, send_sem=ss, recv_sem=rs, device_id=device, device_id_type=MESH
        )

    hw_copy = pltpu.make_async_copy(hw_ref, hwbuf, hw_sem)

    barrier = pltpu.get_barrier_semaphore()

    def plane(p):
        q = lax.rem(x * 8 + t + p, 32)
        return (z * NX + lax.div(q, 8), lax.rem(q, 8))

    def sig_z(d):
        pl.semaphore_signal(barrier, inc=1, device_id=dev(mod(z + d, NZ), x, y, c), device_id_type=MESH)

    def sig_p(p):
        pl.semaphore_signal(barrier, inc=1, device_id=plane(p), device_id_type=MESH)

    fori(1, NZ, sig_z)
    fori(1, 32, sig_p)

    w_in = pltpu.make_async_copy(w_ref, wbuf.at[z], in_sem.at[0])
    w_in.start()
    d_in = pltpu.make_async_copy(dcache_ref, dcv, in_sem.at[1])
    d_in.start()
    p_in = pltpu.make_async_copy(pre_ref, prev, in_sem.at[2])
    p_in.start()
    q_in = pltpu.make_async_copy(q_ref, qv, in_sem.at[3])
    q_in.start()
    hw_copy.start()

    w_in.wait()
    pl.semaphore_wait(barrier, NZ - 1 + 31)

    def w_right(k, j):
        b = wbuf.at[mod(z - k + 1, NZ), pl.ds(j * WR, WR)]
        return rcopy(b, b, wr_s.at[k * NCH + j], wr_r.at[k * NCH + j], dev(mod(z + 1, NZ), x, y, c))

    def w_left(k, j):
        b = wbuf.at[mod(z + k - 1, NZ), pl.ds(j * WR, WR)]
        return rcopy(b, b, wl_s.at[k * NCH + j], wl_r.at[k * NCH + j], dev(mod(z - 1, NZ), x, y, c))

    def w_right_in(k, j):
        b = wbuf.at[mod(z - k, NZ), pl.ds(j * WR, WR)]
        return rcopy(b, b, wr_s.at[k * NCH + j], wr_r.at[k * NCH + j], dev(mod(z + 1, NZ), x, y, c))

    def w_left_in(k, j):
        b = wbuf.at[mod(z + k, NZ), pl.ds(j * WR, WR)]
        return rcopy(b, b, wl_s.at[k * NCH + j], wl_r.at[k * NCH + j], dev(mod(z - 1, NZ), x, y, c))

    def w_forward(k):
        def one(j):
            w_right_in(k, j).wait_recv()
            if k < 8:
                w_right(k + 1, j).start()
                w_left_in(k, j).wait_recv()
            if k < 7:
                w_left(k + 1, j).start()

        fori(0, NCH, one)

    def w_first(j):
        w_right(1, j).start()
        w_left(1, j).start()

    fori(0, NCH, w_first)

    qd[...] = jnp.zeros_like(qd)
    dq = dq_ref[...].astype(F32)
    for r in range(4):
        for h in range(GROUP):
            qd[r * 8 + h : r * 8 + h + 1, :] = dq[r : r + 1, h * HD : (h + 1) * HD]
    qall = qd[...].astype(BF16)
    row = lax.broadcasted_iota(jnp.int32, (32, 1), 0)
    rows_slot = jnp.zeros((32, 1), jnp.int32)
    rows_len = jnp.zeros((32, 1), jnp.int32)
    for r in range(4):
        inside = lax.div(row, 8) == r
        rows_slot = jnp.where(inside, slot_ref[r], rows_slot)
        rows_len = jnp.where(inside, cache_len_ref[r], rows_len)
    d_in.wait()
    keys = dcv[0].reshape(5 * 128, HD)
    vals = dcv[1].reshape(5 * 128, HD)
    col = lax.broadcasted_iota(jnp.int32, (32, 640), 1)
    live = (lax.div(col, 128) == rows_slot) & (s * 128 + lax.rem(col, 128) < rows_len)
    sc = lax.dot_general(qall, keys, NT, preferred_element_type=F32) * scale
    sc = jnp.where(live, sc, NEG)
    dm = jnp.max(sc, axis=-1, keepdims=True)
    dw = jnp.where(live, jnp.exp(sc - dm), 0.0)
    dl = jnp.sum(dw, axis=-1, keepdims=True)
    hi = dw.astype(BF16)
    lo = (dw - hi.astype(F32)).astype(BF16)
    do = jnp.dot(hi, vals, preferred_element_type=F32) + jnp.dot(lo, vals, preferred_element_type=F32)
    lane = lax.broadcasted_iota(jnp.int32, (32, HD), 1)
    dstat = jnp.where(lane < 64, dm, dl)
    for r in range(4):
        dpart[r, 0:8, :] = do[r * 8 : r * 8 + 8]
        dpart[r, 8:16, :] = dstat[r * 8 : r * 8 + 8]

    def dx(d):
        xx = mod(x + d, NX)
        return rcopy(dpart.at[xx], dxb.at[x], dx_s.at[d], dx_r.at[d], dev(z, xx, y, c))

    dxb[x] = dpart[x]
    fori(1, NX, lambda d: dx(d).start())

    pe = prefix_len_ref[s]
    p_in.wait()
    q_in.wait()
    kp, ko = prev[0, 0], kv_ref[0]
    vp, vo = prev[1, 0], kv_ref[1]
    n_pre = kp.shape[0]
    live1 = lax.broadcasted_iota(jnp.int32, (128, n_pre), 1) < pe
    live2 = lax.broadcasted_iota(jnp.int32, (128, 128), 1) <= lax.broadcasted_iota(jnp.int32, (128, 128), 0)
    lrow[...] = jnp.zeros_like(lrow)

    def head(h):
        hs = pl.ds(pl.multiple_of(h * HD, HD), HD)
        qh = qv[:, hs]
        s1 = lax.dot_general(qh, kp, NT, preferred_element_type=F32) * scale
        s2 = lax.dot_general(qh, ko, NT, preferred_element_type=F32) * scale
        s1 = jnp.where(live1, s1, NEG)
        s2 = jnp.where(live2, s2, NEG)
        m = jnp.maximum(jnp.max(s1, -1, keepdims=True), jnp.max(s2, -1, keepdims=True))
        p1 = jnp.where(live1, jnp.exp(s1 - m), 0.0)
        p2 = jnp.where(live2, jnp.exp(s2 - m), 0.0)
        total = jnp.sum(p1, -1, keepdims=True) + jnp.sum(p2, -1, keepdims=True)
        o = jnp.dot(p1.astype(BF16), vp, preferred_element_type=F32)
        o += jnp.dot(p2.astype(BF16), vo, preferred_element_type=F32)
        o = (o / total).astype(BF16)
        abuf[x, :, hs] = o
        lrow[pl.ds(h, 1), :] = o.astype(F32)[127:128, :]
        lrow[pl.ds(8 + h, 1), :] = hid_ref[:, hs].astype(F32)[127:128, :]

    fori(0, 2, head)
    w_forward(1)

    def merge(ref):
        os = [ref[i, 0:8, :] for i in range(4)]
        st = [ref[i, 8:16, :] for i in range(4)]
        ms = [a[:, 0:1] for a in st]
        lls = [a[:, 64:65] for a in st]
        m = jnp.maximum(jnp.maximum(ms[0], ms[1]), jnp.maximum(ms[2], ms[3]))
        o, l = 0.0, 0.0
        for i in range(4):
            f = jnp.exp(ms[i] - m)
            o = o + os[i] * f
            l = l + lls[i] * f
        return o, m, l

    lane8 = lax.broadcasted_iota(jnp.int32, (8, HD), 1)

    def dx_in(d):
        return rcopy(dpart.at[x], dxb.at[mod(x - d, NX)], dx_s.at[d], dx_r.at[d], dev(z, mod(x + d, NX), y, c))

    fori(1, NX, lambda d: dx_in(d).wait_recv())
    o, m, l = merge(dxb)
    zl, zg = lax.rem(z, 4), lax.div(z, 4)
    dz1[zl, 0:8, :] = o
    dz1[zl, 8:16, :] = jnp.where(lane8 < 64, m, l)

    def d1(d, slot):
        return rcopy(dz1.at[slot], dz1.at[slot], d1_s.at[d], d1_r.at[d], dev(zg * 4 + mod(zl + d, 4), x, y, c))

    fori(1, 4, lambda d: d1(d, zl).start())
    fori(2, GROUP, head)

    def a_copy(d, src):
        return rcopy(abuf.at[src], abuf.at[src], a_s.at[d], a_r.at[d], dev(z, mod(x + d, NX), y, c))

    def gz(d, slot):
        return rcopy(agz.at[slot], agz.at[slot], gz_s.at[d], gz_r.at[d], dev(mod(z + d, NZ), x, y, c))

    agz[z] = lrow[...].astype(BF16)
    fori(1, NZ, lambda d: gz(d, z).start())
    w_forward(2)
    fori(1, NX, lambda d: a_copy(d, x).start())
    fori(1, 4, lambda d: d1(d, mod(zl - d, 4)).wait_recv())
    o, m, l = merge(dz1)
    dz2[zg, 0:8, :] = o
    dz2[zg, 8:16, :] = jnp.where(lane8 < 64, m, l)

    def d2(d, slot):
        return rcopy(dz2.at[slot], dz2.at[slot], d2_s.at[d], d2_r.at[d], dev(mod(zg + d, 4) * 4 + zl, x, y, c))

    fori(1, 4, lambda d: d2(d, zg).start())
    w_forward(3)
    w_forward(4)
    w_forward(5)

    fori(1, NZ, lambda d: gz(d, mod(z - d, NZ)).wait_recv())
    for i in range(NZ):
        rows[i * 16 : i * 16 + 16, :] = agz[i].astype(F32)
    mine16 = pl.ds(pl.multiple_of(x * 32, 16), 16)
    for h in range(GROUP):
        hs = slice(h * HD, (h + 1) * HD)
        dmat[mine16, hs] = rows[pl.ds(h, NZ, stride=16), :].astype(BF16)
        hres[0:16, hs] = rows[pl.ds(8 + h, NZ, stride=16), :]

    def lx(d, xx):
        ref = dmat.at[pl.ds(pl.multiple_of(xx * 32, 16), 16)]
        return rcopy(ref, ref, lx_s.at[d], lx_r.at[d], dev(z, mod(x + d, NX), y, c))

    fori(1, NX, lambda d: lx(d, x).start())
    w_forward(6)
    fori(1, 4, lambda d: d2(d, mod(zg - d, 4)).wait_recv())
    o, m, l = merge(dz2)
    row4 = lax.broadcasted_iota(jnp.int32, (4, HD), 0)
    own_k = jnp.sum(jnp.where(row4 == x, dkv_ref[0].astype(F32), 0.0), axis=0, keepdims=True)
    own_v = jnp.sum(jnp.where(row4 == x, dkv_ref[1].astype(F32), 0.0), axis=0, keepdims=True)
    own_q = qd[pl.ds(pl.multiple_of(x * 8, 8), 8), :]
    own_s = jnp.sum(own_q * own_k, axis=-1, keepdims=True) * scale
    m2 = jnp.maximum(m, own_s)
    f1, f2 = jnp.exp(m - m2), jnp.exp(own_s - m2)
    dfin[x] = (o * f1 + own_v * f2) / (l * f1 + f2)

    def df(d, slot):
        return rcopy(dfin.at[slot], dfin.at[slot], df_s.at[d], df_r.at[d], dev(z, mod(x + d, NX), y, c))

    fori(1, NX, lambda d: df(d, x).start())
    w_forward(7)
    fori(1, NX, lambda d: a_copy(d, mod(x - d, NX)).wait_recv())
    fori(1, NX, lambda d: lx(d, mod(x - d, NX)).wait_recv())
    fori(1, NX, lambda d: df(d, mod(x - d, NX)).wait_recv())
    dtmp[...] = jnp.zeros_like(dtmp)
    for r in range(4):
        for h in range(GROUP):
            dtmp[r : r + 1, h * HD : (h + 1) * HD] = dfin[r, h : h + 1, :]
    for xx in range(NX):
        dmat[xx * 32 + 16 : xx * 32 + 32, :] = dtmp[...].astype(BF16)
    hs_buf[...] = jnp.zeros_like(hs_buf)
    ho_buf[...] = jnp.zeros_like(ho_buf)
    w_forward(8)

    def head_product(g, cc, dst):
        for j in range(2):
            p = lax.dot_general(dmat[...], wbuf[g * 4 + cc * 2 + j], NT, preferred_element_type=F32)
            for xx in range(NX):
                dst[xx, j * 32 : j * 32 + 32, 0:WC] = p[xx * 32 : xx * 32 + 32]

    def hx(d):
        return rcopy(hs_buf.at[d], hr_buf.at[d], hx_s.at[d], hx_r.at[d], dev(z, x, y, 1 - c))

    def head_other(d):
        head_product(mod(y + d, NY), 1 - c, hs_buf.at[d])
        hx(d).start()

    fori(0, NY, head_other)
    fori(0, NY, lambda d: head_product(mod(y + d, NY), c, ho_buf.at[d]))

    def hm(d, xx):
        return rcopy(
            hmsg.at[d, xx],
            hrb.at[x * 4 + y],
            hm_s.at[d * 4 + xx],
            hm_r.at[x * 4 + y],
            dev(z, xx, mod(y + d, NY), c),
        )

    def away(fn):
        def each(d, xx):
            @pl.when((d != 0) | (xx != x))
            def _():
                fn(d, xx)

        return lambda i: each(lax.div(i, 4), lax.rem(i, 4))

    def head_send(i):
        d = lax.rem(i + 1, NY)
        hx(d).wait_recv()
        hmsg[d] = (ho_buf[d] + hr_buf[d]).astype(BF16)
        fori(d * 4, d * 4 + 4, away(lambda d, xx: hm(d, xx).start()))

    fori(0, NY, head_send)
    hrb[x * 4 + y] = hmsg[0, x]

    def product(g, cc, main):
        a = abuf[...].reshape(4 * 128, KW)
        wt = wbuf[pl.ds(g * 4 + cc * 2, 2)].reshape(2 * WC, KW)
        main[...] = lax.dot_general(wt, a, NT, preferred_element_type=F32)

    def cm(d):
        return rcopy(cs_main.at[d], cr_main.at[d], cm_s.at[d], cm_r.at[d], dev(z, x, y, 1 - c))

    def make(d):
        product(mod(y + d, NY), 1 - c, cs_main.at[d])
        cm(d).start()

    fori(0, NY, make)

    def hm_in(p):
        src = lax.rem(x * 4 + y + p, 16)
        return rcopy(hmsg.at[0, 0], hrb.at[src], hm_s.at[0], hm_r.at[src], dev(z, x, y, 1 - c))

    fori(1, 16, lambda p: hm_in(p).wait_recv())
    hlane = lax.broadcasted_iota(jnp.int32, (32, HD), 1)
    hproj = jnp.zeros((32, KW), F32)
    for xs in range(NX):
        tot = hrb[xs * 4].astype(F32)
        for ys in range(1, NY):
            tot += hrb[xs * 4 + ys].astype(F32)
        for j in range(2):
            blk = j * 4 + xs
            piece = jnp.where(hlane < WC, tot[j * 32 : j * 32 + 32, :], 0.0)
            wide = jnp.concatenate([piece, jnp.zeros((32, KW - HD), F32)], axis=1)
            hproj += pltpu.roll(wide, blk * WC, 1) if blk else wide

    def drows(tt):
        return hbuf.at[pl.ds(64, 16), pl.ds(pl.multiple_of(tt * KW, HD), KW)]

    def hrows(xx, tt):
        return hbuf.at[pl.ds(pl.multiple_of(xx * 16, 16), 16), pl.ds(pl.multiple_of(tt * KW, HD), KW)]

    hrows(x, t)[...] = (hres[0:16, :] + hproj[0:16]).astype(BF16)

    def hbc(p, i):
        q = lax.rem(x * 4 + y + p, 16)
        ref = hrows(lax.div(i, 4), lax.rem(i, 4) * NC + c)
        return rcopy(ref, ref, hb_s.at[p], hb_r.at[p], dev(z, lax.div(q, 4), lax.rem(q, 4), c))

    def hcc(p, i, cc):
        ref = hrows(lax.div(i, 4), lax.rem(i, 4) * NC + cc)
        return rcopy(ref, ref, hc_s.at[p], hc_r.at[p], dev(z, x, y, 1 - c))

    def dbc(d, yy):
        ref = drows(yy * NC + c)
        return rcopy(ref, ref, db_s.at[d], db_r.at[d], dev(z, x, mod(y + d, NY), c))

    def dcc(d, yy, cc):
        ref = drows(yy * NC + cc)
        return rcopy(ref, ref, dc_s.at[d], dc_r.at[d], dev(z, x, y, 1 - c))

    fori(1, 16, lambda p: hbc(p, x * 4 + y).start())
    hcc(0, x * 4 + y, c).start()
    dres = (dhid_ref[...].astype(F32) + hproj[16:20]).astype(BF16)
    dout_ref[...] = dres
    drows(t)[...] = jnp.concatenate([dres.astype(F32), jnp.zeros((12, KW), F32)], axis=0).astype(BF16)
    fori(1, NY, lambda d: dbc(d, y).start())
    dcc(0, y, c).start()

    fori(0, NY, lambda d: product(mod(y + d, NY), c, co_main.at[d]))

    def finish(d):
        cm(d).wait_recv()
        for xx in range(NX):
            ls = slice(xx * 128, (xx + 1) * 128)
            msg[d * 4 + xx] = (co_main[d, :, ls] + cr_main[d, :, ls]).astype(BF16)

    fori(0, NY, finish)

    def hfwd(p):
        i = lax.rem(x * 4 + y - p + 16, 16)
        hbc(p, i).wait_recv()
        hcc(p, i, c).start()

    fori(1, 16, hfwd)

    def dfwd(d):
        yy = mod(y - d, NY)
        dbc(d, yy).wait_recv()
        dcc(d, yy, c).start()

    fori(1, NY, dfwd)

    def r_copy(d, xx):
        return rcopy(
            msg.at[d * 4 + xx],
            rbuf.at[x * 4 + y],
            r_s.at[d * 4 + xx],
            r_r.at[x * 4 + y],
            dev(z, xx, mod(y + d, NY), c),
        )

    fori(4, 20, lambda i: away(lambda d, xx: r_copy(d, xx).start())(lax.rem(i, 16)))
    rbuf[x * 4 + y] = msg[x]
    fori(0, NY, lambda d: dcc(d, mod(y - d, NY), 1 - c).wait_recv())
    fori(0, 16, lambda p: hcc(p, lax.rem(x * 4 + y - p + 16, 16), 1 - c).wait_recv())
    hw_copy.wait()

    def chunk(i):
        return pl.ds(pl.multiple_of(i * KW, HD), KW)

    def square(i, acc):
        v = hbuf[:, chunk(i)].astype(F32)
        return acc + jnp.sum(v * v, axis=-1, keepdims=True)

    ssq = lax.fori_loop(0, 8, square, jnp.zeros((80, 1), F32))
    inv = lax.rsqrt(ssq / 5120.0 + EPS)
    vocab = hwbuf.shape[0]

    def logit(i, acc):
        v = hbuf[:, chunk(i)].astype(F32)
        n = (v * inv * gain_ref[:, chunk(i)].astype(F32)).astype(BF16)
        return acc + lax.dot_general(n, hwbuf[:, chunk(i)], NT, preferred_element_type=F32)

    logits = lax.fori_loop(0, 8, logit, jnp.zeros((80, vocab), F32))
    lm = jnp.max(logits, axis=-1, keepdims=True)
    ll = jnp.sum(jnp.exp(logits - lm), axis=-1, keepdims=True)

    ln = lax.broadcasted_iota(jnp.int32, (80, HD), 1)
    tmat[...] = jnp.zeros_like(tmat)
    tmat[0:80, :] = jnp.where(ln == 0, lm, jnp.where(ln == 1, ll, 0.0))
    me = x * 8 + t
    lsz[z] = tmat[...].T[0:8, :]

    def lzc(d, i):
        return rcopy(lsz.at[i], lsz.at[i], lz_s.at[d], lz_r.at[d], dev(mod(z + d, NZ), x, y, c))

    def lsc(p, i):
        return rcopy(lst.at[i], lst.at[i], ls_s.at[p], ls_r.at[p], plane(p))

    def join(ref, n):
        f = ref.reshape(n * 8, HD)
        ms = f[pl.ds(0, n, stride=8), :]
        lls = f[pl.ds(1, n, stride=8), :]
        top = jnp.max(ms, axis=0, keepdims=True)
        return top, jnp.sum(lls * jnp.exp(ms - top), axis=0, keepdims=True)

    fori(1, NZ, lambda d: lzc(d, z).start())

    def r_in(p):
        src = lax.rem(x * 4 + y + p, 16)
        return rcopy(msg.at[0], rbuf.at[src], r_s.at[0], r_r.at[src], dev(z, x, y, 1 - c))

    fori(1, 16, lambda p: r_in(p).wait_recv())
    for xs in range(NX):
        tot = rbuf[xs * 4].astype(F32)
        for ys in range(1, NY):
            tot += rbuf[xs * 4 + ys].astype(F32)
        for j in range(2):
            blk = j * 4 + xs
            big[blk * WC : (blk + 1) * WC, :] = tot[j * WC : (j + 1) * WC, :]
    for h in range(GROUP):
        ls = slice(h * HD, (h + 1) * HD)
        out_ref[:, ls] = (hid_ref[:, ls].astype(F32) + big[ls, :].T).astype(BF16)

    fori(1, NZ, lambda d: lzc(d, mod(z - d, NZ)).wait_recv())
    top, tot = join(lsz, NZ)
    r8 = lax.broadcasted_iota(jnp.int32, (8, HD), 0)
    lst[me] = jnp.where(r8 == 0, top, tot)
    fori(1, 32, lambda p: lsc(p, me).start())
    fori(1, 32, lambda p: lsc(p, lax.rem(me - p + 32, 32)).wait_recv())
    top, tot = join(lst, 32)
    tmat[...] = jnp.broadcast_to(top + jnp.log(tot), (HD, HD))
    lse = tmat[...].T[0:80, 0:1]
    lp = logits - lse
    lp_ref[0:4, :] = lp[64:68]
    for i in range(64):
        xx, zz = i // 16, i % 16
        lp_ref[4 + zz * 4 + xx : 5 + zz * 4 + xx, :] = lp[i : i + 1]

    def ring(i):
        w_right(lax.div(i, NCH), lax.rem(i, NCH)).wait_send()

        @pl.when(i < 8 * NCH)
        def _():
            w_left(lax.div(i, NCH), lax.rem(i, NCH)).wait_send()

    fori(NCH, 9 * NCH, ring)

    def three(d):
        dx(d).wait_send()
        a_copy(d, x).wait_send()
        lx(d, x).wait_send()
        d1(d, zl).wait_send()
        d2(d, zg).wait_send()
        df(d, x).wait_send()
        dbc(d, y).wait_send()

    fori(1, 4, three)

    def four(d):
        hx(d).wait_send()
        cm(d).wait_send()
        dcc(d, mod(y - d, NY), c).wait_send()

    fori(0, 4, four)

    def leave(d, xx):
        hm(d, xx).wait_send()
        r_copy(d, xx).wait_send()

    fori(0, 16, away(leave))

    def fifteen(d):
        gz(d, z).wait_send()
        hbc(d, x * 4 + y).wait_send()
        lzc(d, z).wait_send()

    fori(1, 16, fifteen)
    fori(0, 16, lambda p: hcc(p, lax.rem(x * 4 + y - p + 16, 16), c).wait_send())
    fori(1, 32, lambda p: lsc(p, me).wait_send())


def local(
    prefill_hidden,
    prefill_query_rows,
    prefill_key_value,
    request_prefix_cache,
    prefix_lengths,
    decode_hidden,
    decode_query_rows,
    decode_kv,
    decode_slot_cache,
    cache_lengths,
    slot_table,
    out_weight,
    final_gain,
    head_weight,
):
    vocab = head_weight.shape[1]
    vm = pl.BlockSpec(memory_space=pltpu.VMEM)
    sm = pl.BlockSpec(memory_space=pltpu.SMEM)
    hbm = pl.BlockSpec(memory_space=pl.ANY)
    dma = lambda n: pltpu.SemaphoreType.DMA((n,))
    sems = []
    for n in (9 * NCH, 8 * NCH, 4, 4, 4, 4, 4, 4, 4, 16, 4, 16, 16, 16, 16, 4, 4, 32, 16):
        sems += [dma(n), dma(n)]
    return pl.pallas_call(
        kernel,
        out_shape=(
            jax.ShapeDtypeStruct((128, KW), BF16),
            jax.ShapeDtypeStruct((4, KW), BF16),
            jax.ShapeDtypeStruct((68, vocab), F32),
        ),
        in_specs=[sm, sm, sm, vm, hbm, vm, hbm, vm, vm, vm, hbm, hbm, vm, hbm],
        out_specs=(vm, vm, vm),
        scratch_shapes=[
            pltpu.VMEM(head_weight.shape[::-1], BF16),
            pltpu.VMEM((NZ, WC, KW), BF16),
            pltpu.VMEM((NX, 128, KW), BF16),
            pltpu.VMEM((32, HD), F32),
            pltpu.VMEM((4, 16, HD), F32),
            pltpu.VMEM((4, 16, HD), F32),
            pltpu.VMEM((4, 16, HD), F32),
            pltpu.VMEM((4, 16, HD), F32),
            pltpu.VMEM((4, 8, HD), F32),
            pltpu.VMEM((128, KW), BF16),
            pltpu.VMEM((16, KW), F32),
            pltpu.VMEM((16, HD), F32),
            pltpu.VMEM((NZ * 16, HD), F32),
            pltpu.VMEM((16, KW), F32),
            pltpu.VMEM((NY, NX, 64, HD), F32),
            pltpu.VMEM((NY, NX, 64, HD), F32),
            pltpu.VMEM((NY, NX, 64, HD), F32),
            pltpu.VMEM((NY, NX, 64, HD), BF16),
            pltpu.VMEM((16, 64, HD), BF16),
            pltpu.VMEM((4, 160, 512), F32),
            pltpu.VMEM((4, 160, 512), F32),
            pltpu.VMEM((4, 160, 512), F32),
            pltpu.VMEM((16, 160, HD), BF16),
            pltpu.VMEM((16, 160, HD), BF16),
            pltpu.VMEM((KW, HD), F32),
            pltpu.VMEM((NZ, 16, HD), BF16),
            pltpu.VMEM((80, 5120), BF16),
            pltpu.VMEM((HD, HD), F32),
            pltpu.VMEM((32, 8, HD), F32),
            pltpu.VMEM((NZ, 8, HD), F32),
            pltpu.VMEM((128, KW), BF16),
            pltpu.VMEM((2, 1, 768, HD), BF16),
            pltpu.VMEM((2, 5, 128, HD), BF16),
            pltpu.SemaphoreType.DMA,
            dma(4),
            *sems,
        ],
        compiler_params=pltpu.CompilerParams(
            collective_id=0, has_side_effects=True, vmem_limit_bytes=60 * 1024 * 1024
        ),
    )(
        prefix_lengths,
        cache_lengths,
        slot_table,
        prefill_hidden,
        prefill_query_rows,
        prefill_key_value,
        request_prefix_cache,
        decode_hidden,
        decode_query_rows,
        decode_kv,
        decode_slot_cache,
        out_weight.T,
        final_gain.reshape(1, -1),
        head_weight.T,
    )


def solution(mesh):
    return jax.shard_map(
        local,
        mesh=mesh,
        in_specs=(
            P("seq", "tp"),
            P("seq", "tp"),
            P(None, "seq", "tp"),
            P(None, "seq", None, "tp"),
            P(),
            P(None, "tp"),
            P(None, "tp"),
            P(None, None, "tp"),
            P(None, None, "seq", "tp"),
            P(),
            P(),
            P("tp", "seq"),
            P(),
            P(None, ("seq", "tp")),
        ),
        out_specs=(P("seq", "tp"), P(None, "tp"), P(None, ("seq", "tp"))),
        check_vma=False,
    )
```

```python
import math

import jax
import jax.numpy as jnp
from jax import lax
from jax.experimental import pallas as pl
from jax.experimental.pallas import tpu as pltpu
from jax.sharding import PartitionSpec as P

NEG = -1e30
EPS = 1e-6
NT = (((1,), (1,)), ((), ()))
MESH = pl.DeviceIdType.MESH
F32 = jnp.float32
BF16 = jnp.bfloat16

NX, NY, NZ, NC = 4, 4, 16, 2
NCH = 5
WR = 16
WC = 80
HD = 128
GROUP = 5
KW = 640


def fori(lo, hi, body):
    def step(i, carry):
        body(i)
        return carry

    lax.fori_loop(lo, hi, step, 0)


def mod(a, n):
    return lax.rem(a + n, n)


def kernel(
    prefix_len_hbm,
    cache_len_hbm,
    slot_hbm,
    hid_hbm,
    q_hbm,
    kv_hbm,
    pre_hbm,
    dhid_hbm,
    dq_hbm,
    dkv_hbm,
    dcache_hbm,
    w_hbm,
    gain_hbm,
    hw_hbm,
    out_ref,
    dout_ref,
    lp_ref,
    hwbuf,
    wbuf,
    abuf,
    qd,
    dpart,
    dxb,
    dz1,
    dz2,
    dfin,
    dmat,
    dtmp,
    lrow,
    rows,
    hres,
    h_buf,
    hr_buf,
    hmsg,
    hrb,
    cs_main,
    cr_main,
    msg,
    rbuf,
    big,
    agz,
    hbuf,
    tmat,
    lst,
    lsz,
    lpad,
    qv,
    prev,
    dcv,
    prefix_len_ref,
    cache_len_ref,
    slot_ref,
    hid_ref,
    kv_ref,
    dhid_ref,
    dq_ref,
    dkv_ref,
    gain_ref,
    gain2,
    in_sem,
    wr_s,
    wr_r,
    wl_s,
    wl_r,
    a_s,
    a_r,
    dx_s,
    dx_r,
    d1_s,
    d1_r,
    d2_s,
    d2_r,
    df_s,
    df_r,
    lx_s,
    lx_r,
    hx_s,
    hx_r,
    hm_s,
    hm_r,
    cm_s,
    cm_r,
    r_s,
    r_r,
    gz_s,
    gz_r,
    hb_s,
    hb_r,
    hc_s,
    hc_r,
    db_s,
    db_r,
    dc_s,
    dc_r,
    ls_s,
    ls_r,
    lz_s,
    lz_r,
):
    s = lax.axis_index("seq")
    t = lax.axis_index("tp")
    z, x = lax.div(s, NX), lax.rem(s, NX)
    y, c = lax.div(t, NC), lax.rem(t, NC)
    scale = 1.0 / math.sqrt(HD)

    def dev(zz, xx, yy, cc):
        return (zz * NX + xx, yy * NC + cc)

    def rcopy(src, dst, ss, rs, device):
        return pltpu.make_async_remote_copy(
            src_ref=src, dst_ref=dst, send_sem=ss, recv_sem=rs, device_id=device, device_id_type=MESH
        )

    barrier = pltpu.get_barrier_semaphore()

    def plane(p):
        q = lax.rem(x * 8 + t + p, 32)
        return (z * NX + lax.div(q, 8), lax.rem(q, 8))

    def sig_z(d):
        pl.semaphore_signal(barrier, inc=1, device_id=dev(mod(z + d, NZ), x, y, c), device_id_type=MESH)

    def sig_p(p):
        pl.semaphore_signal(barrier, inc=1, device_id=plane(p), device_id_type=MESH)

    fori(1, NZ, sig_z)
    fori(1, 32, sig_p)

    def bring(i, src, dst):
        copy = pltpu.make_async_copy(src, dst, in_sem.at[i])
        copy.start()
        return copy

    w_in = bring(0, w_hbm, wbuf.at[z])
    dq_in = bring(1, dq_hbm, dq_ref)
    slot_in = bring(2, slot_hbm, slot_ref)
    clen_in = bring(3, cache_len_hbm, cache_len_ref)
    d_in = bring(4, dcache_hbm, dcv)
    plen_in = bring(5, prefix_len_hbm, prefix_len_ref)
    p_in = bring(6, pre_hbm, prev)
    q_in = bring(7, q_hbm, qv)
    kv_in = bring(8, kv_hbm, kv_ref)
    hid_in = bring(9, hid_hbm, hid_ref)
    dkv_in = bring(10, dkv_hbm, dkv_ref)
    dhid_in = bring(11, dhid_hbm, dhid_ref)
    gain_in = bring(12, gain_hbm, gain_ref)
    hw_copy = bring(13, hw_hbm, hwbuf)
    w_in.wait()
    pl.semaphore_wait(barrier, NZ - 1 + 31)

    def w_right(k, j):
        b = wbuf.at[mod(z - k + 1, NZ), pl.ds(j * WR, WR)]
        return rcopy(b, b, wr_s.at[k * NCH + j], wr_r.at[k * NCH + j], dev(mod(z + 1, NZ), x, y, c))

    def w_left(k, j):
        b = wbuf.at[mod(z + k - 1, NZ), pl.ds(j * WR, WR)]
        return rcopy(b, b, wl_s.at[k * NCH + j], wl_r.at[k * NCH + j], dev(mod(z - 1, NZ), x, y, c))

    def w_right_in(k, j):
        b = wbuf.at[mod(z - k, NZ), pl.ds(j * WR, WR)]
        return rcopy(b, b, wr_s.at[k * NCH + j], wr_r.at[k * NCH + j], dev(mod(z + 1, NZ), x, y, c))

    def w_left_in(k, j):
        b = wbuf.at[mod(z + k, NZ), pl.ds(j * WR, WR)]
        return rcopy(b, b, wl_s.at[k * NCH + j], wl_r.at[k * NCH + j], dev(mod(z - 1, NZ), x, y, c))

    def w_forward(k):
        def one(j):
            w_right_in(k, j).wait_recv()
            w_right(k + 1, j).start()
            w_left_in(k, j).wait_recv()
            w_left(k + 1, j).start()

        def turn(j):
            w_right_in(7, j).wait_recv()
            w_left_in(7, j).wait_recv()

            @pl.when(j < 3)
            def _():
                w_right(8, j).start()

            @pl.when(j >= 3)
            def _():
                w_left(8, j).start()

        def last(j):
            @pl.when(j < 3)
            def _():
                w_right_in(8, j).wait_recv()

            @pl.when(j >= 3)
            def _():
                w_left_in(8, j).wait_recv()

        fori(0, NCH, one if k < 7 else turn if k == 7 else last)

    def w_first(j):
        w_right(1, j).start()
        w_left(1, j).start()

    fori(0, NCH, w_first)

    qd[...] = jnp.zeros_like(qd)
    dq_in.wait()
    slot_in.wait()
    clen_in.wait()
    dq = dq_ref[...].astype(F32)
    for r in range(4):
        for h in range(GROUP):
            qd[r * 8 + h : r * 8 + h + 1, :] = dq[r : r + 1, h * HD : (h + 1) * HD]
    qall = qd[...].astype(BF16)
    row = lax.broadcasted_iota(jnp.int32, (32, 1), 0)
    rows_slot = jnp.zeros((32, 1), jnp.int32)
    rows_len = jnp.zeros((32, 1), jnp.int32)
    for r in range(4):
        inside = lax.div(row, 8) == r
        rows_slot = jnp.where(inside, slot_ref[r], rows_slot)
        rows_len = jnp.where(inside, cache_len_ref[r], rows_len)
    d_in.wait()
    keys = dcv[0].reshape(5 * 128, HD)
    vals = dcv[1].reshape(5 * 128, HD)
    col = lax.broadcasted_iota(jnp.int32, (32, 640), 1)
    live = (lax.div(col, 128) == rows_slot) & (s * 128 + lax.rem(col, 128) < rows_len)
    sc = lax.dot_general(qall, keys, NT, preferred_element_type=F32) * scale
    sc = jnp.where(live, sc, NEG)
    dm = jnp.max(sc, axis=-1, keepdims=True)
    dw = jnp.where(live, jnp.exp(sc - dm), 0.0)
    dl = jnp.sum(dw, axis=-1, keepdims=True)
    hi = dw.astype(BF16)
    lo = (dw - hi.astype(F32)).astype(BF16)
    do = jnp.dot(hi, vals, preferred_element_type=F32) + jnp.dot(lo, vals, preferred_element_type=F32)
    lane = lax.broadcasted_iota(jnp.int32, (32, HD), 1)
    dstat = jnp.where(lane < 64, dm, dl)
    for r in range(4):
        dpart[r, 0:8, :] = do[r * 8 : r * 8 + 8]
        dpart[r, 8:16, :] = dstat[r * 8 : r * 8 + 8]

    def dx(d):
        xx = mod(x + d, NX)
        return rcopy(dpart.at[xx], dxb.at[x], dx_s.at[d], dx_r.at[d], dev(z, xx, y, c))

    dxb[x] = dpart[x]
    fori(1, NX, lambda d: dx(d).start())

    plen_in.wait()
    p_in.wait()
    q_in.wait()
    kv_in.wait()
    hid_in.wait()
    pe = prefix_len_ref[s]
    kp, ko = prev[0, 0], kv_ref[0]
    vp, vo = prev[1, 0], kv_ref[1]
    n_pre = kp.shape[0]
    live1 = lax.broadcasted_iota(jnp.int32, (128, n_pre), 1) < pe
    live2 = lax.broadcasted_iota(jnp.int32, (128, 128), 1) <= lax.broadcasted_iota(jnp.int32, (128, 128), 0)
    lrow[...] = jnp.zeros_like(lrow)

    def head(h):
        hs = pl.ds(pl.multiple_of(h * HD, HD), HD)
        qh = qv[:, hs]
        s1 = lax.dot_general(qh, kp, NT, preferred_element_type=F32) * scale
        s2 = lax.dot_general(qh, ko, NT, preferred_element_type=F32) * scale
        s1 = jnp.where(live1, s1, NEG)
        s2 = jnp.where(live2, s2, NEG)
        m = jnp.maximum(jnp.max(s1, -1, keepdims=True), jnp.max(s2, -1, keepdims=True))
        p1 = jnp.where(live1, jnp.exp(s1 - m), 0.0)
        p2 = jnp.where(live2, jnp.exp(s2 - m), 0.0)
        total = jnp.sum(p1, -1, keepdims=True) + jnp.sum(p2, -1, keepdims=True)
        o = jnp.dot(p1.astype(BF16), vp, preferred_element_type=F32)
        o += jnp.dot(p2.astype(BF16), vo, preferred_element_type=F32)
        o = (o / total).astype(BF16)
        abuf[x, :, hs] = o
        lrow[pl.ds(h, 1), :] = o.astype(F32)[127:128, :]
        lrow[pl.ds(8 + h, 1), :] = hid_ref[:, hs].astype(F32)[127:128, :]


    def merge(ref):
        os = [ref[i, 0:8, :] for i in range(4)]
        st = [ref[i, 8:16, :] for i in range(4)]
        ms = [a[:, 0:1] for a in st]
        lls = [a[:, 64:65] for a in st]
        m = jnp.maximum(jnp.maximum(ms[0], ms[1]), jnp.maximum(ms[2], ms[3]))
        o, l = 0.0, 0.0
        for i in range(4):
            f = jnp.exp(ms[i] - m)
            o = o + os[i] * f
            l = l + lls[i] * f
        return o, m, l

    lane8 = lax.broadcasted_iota(jnp.int32, (8, HD), 1)

    def dx_in(d):
        return rcopy(dpart.at[x], dxb.at[mod(x - d, NX)], dx_s.at[d], dx_r.at[d], dev(z, mod(x + d, NX), y, c))

    zl, zg = lax.rem(z, 4), lax.div(z, 4)
    def heads(h):
        head(h)

        @pl.when(h == 2)
        def _():
            w_forward(1)

    fori(0, GROUP, heads)
    fori(1, NX, lambda d: dx_in(d).wait_recv())
    o, m, l = merge(dxb)
    dz1[zl, 0:8, :] = o
    dz1[zl, 8:16, :] = jnp.where(lane8 < 64, m, l)

    def d1(d, slot):
        return rcopy(dz1.at[slot], dz1.at[slot], d1_s.at[d], d1_r.at[d], dev(zg * 4 + mod(zl + d, 4), x, y, c))

    fori(1, 4, lambda d: d1(d, zl).start())

    def a_copy(d, src):
        return rcopy(abuf.at[src], abuf.at[src], a_s.at[d], a_r.at[d], dev(z, mod(x + d, NX), y, c))

    def gz(d, slot):
        return rcopy(agz.at[slot], agz.at[slot], gz_s.at[d], gz_r.at[d], dev(mod(z + d, NZ), x, y, c))

    agz[z] = lrow[...].astype(BF16)
    fori(1, NZ, lambda d: gz(d, z).start())
    w_forward(2)
    fori(1, NX, lambda d: a_copy(d, x).start())
    fori(1, 4, lambda d: d1(d, mod(zl - d, 4)).wait_recv())
    o, m, l = merge(dz1)
    dz2[zg, 0:8, :] = o
    dz2[zg, 8:16, :] = jnp.where(lane8 < 64, m, l)

    def d2(d, slot):
        return rcopy(dz2.at[slot], dz2.at[slot], d2_s.at[d], d2_r.at[d], dev(mod(zg + d, 4) * 4 + zl, x, y, c))

    fori(1, 4, lambda d: d2(d, zg).start())
    w_forward(3)
    w_forward(4)
    w_forward(5)

    fori(1, NZ, lambda d: gz(d, mod(z - d, NZ)).wait_recv())
    for i in range(NZ):
        rows[i * 16 : i * 16 + 16, :] = agz[i].astype(F32)
    mine16 = pl.ds(pl.multiple_of(x * 32, 16), 16)
    for h in range(GROUP):
        hs = slice(h * HD, (h + 1) * HD)
        dmat[mine16, hs] = rows[pl.ds(h, NZ, stride=16), :].astype(BF16)
        hres[0:16, hs] = rows[pl.ds(8 + h, NZ, stride=16), :]

    def lx(d, xx):
        ref = dmat.at[pl.ds(pl.multiple_of(xx * 32, 16), 16)]
        return rcopy(ref, ref, lx_s.at[d], lx_r.at[d], dev(z, mod(x + d, NX), y, c))

    fori(1, NX, lambda d: lx(d, x).start())
    w_forward(6)
    fori(1, 4, lambda d: d2(d, mod(zg - d, 4)).wait_recv())
    o, m, l = merge(dz2)
    dkv_in.wait()
    row4 = lax.broadcasted_iota(jnp.int32, (4, HD), 0)
    own_k = jnp.sum(jnp.where(row4 == x, dkv_ref[0].astype(F32), 0.0), axis=0, keepdims=True)
    own_v = jnp.sum(jnp.where(row4 == x, dkv_ref[1].astype(F32), 0.0), axis=0, keepdims=True)
    own_q = qd[pl.ds(pl.multiple_of(x * 8, 8), 8), :]
    own_s = jnp.sum(own_q * own_k, axis=-1, keepdims=True) * scale
    m2 = jnp.maximum(m, own_s)
    f1, f2 = jnp.exp(m - m2), jnp.exp(own_s - m2)
    dfin[x] = (o * f1 + own_v * f2) / (l * f1 + f2)

    def df(d, slot):
        return rcopy(dfin.at[slot], dfin.at[slot], df_s.at[d], df_r.at[d], dev(z, mod(x + d, NX), y, c))

    fori(1, NX, lambda d: df(d, x).start())
    w_forward(7)
    fori(1, NX, lambda d: a_copy(d, mod(x - d, NX)).wait_recv())
    fori(1, NX, lambda d: lx(d, mod(x - d, NX)).wait_recv())
    fori(1, NX, lambda d: df(d, mod(x - d, NX)).wait_recv())
    dtmp[...] = jnp.zeros_like(dtmp)
    for r in range(4):
        for h in range(GROUP):
            dtmp[r : r + 1, h * HD : (h + 1) * HD] = dfin[r, h : h + 1, :]
    for xx in range(NX):
        dmat[xx * 32 + 16 : xx * 32 + 32, :] = dtmp[...].astype(BF16)
    h_buf[...] = jnp.zeros_like(h_buf)

    def head_product(e, i):
        p = lax.dot_general(dmat[...], wbuf[mod(zg + e, NY) * 4 + i], NT, preferred_element_type=F32)
        half = pl.ds(pl.multiple_of(lax.rem(i, 2) * 32, 32), 32)
        for xx in range(NX):
            h_buf[e, lax.div(i, 2), xx, half, 0:WC] = p[xx * 32 : xx * 32 + 32]

    def hx(e):
        return rcopy(h_buf.at[e, 1 - c], hr_buf.at[e], hx_s.at[e], hx_r.at[e], dev(z, x, y, 1 - c))

    def head_group(e):
        fori(0, 4, lambda i: head_product(e, i))
        hx(e).start()

    def hm(e, xx):
        return rcopy(
            hmsg.at[e, xx],
            hrb.at[x * 4 + y],
            hm_s.at[e * 4 + xx],
            hm_r.at[x * 4 + y],
            dev(z, xx, mod(zg + e, NY), c),
        )

    def away_head(fn):
        def each(e, xx):
            @pl.when((mod(zg + e, NY) != y) | (xx != x))
            def _():
                fn(e, xx)

        return lambda i: each(lax.div(i, 4), lax.rem(i, 4))

    def head_send(e):
        hx(e).wait_recv()
        hmsg[e] = (h_buf[e, c] + hr_buf[e]).astype(BF16)
        fori(e * 4, e * 4 + 4, away_head(lambda e, xx: hm(e, xx).start()))

    def head_step(i):
        @pl.when(i == 3)
        def _():
            w_forward(8)

        head_group(i + lax.div(i, 2) - 2 * lax.div(i, 3))

    fori(0, 4, head_step)
    fori(0, 4, lambda i: head_send(i + lax.div(i, 2) - 2 * lax.div(i, 3)))
    hrb[x * 4 + y] = hmsg[mod(y - zg, NY), x]

    def away(fn):
        def each(d, xx):
            @pl.when((d != 0) | (xx != x))
            def _():
                fn(d, xx)

        return lambda i: each(lax.div(i, 4), lax.rem(i, 4))

    half_other = pl.ds(pl.multiple_of((1 - c) * 160, 8), 160)
    half_mine = pl.ds(pl.multiple_of(c * 160, 8), 160)

    def cm(d):
        return rcopy(cs_main.at[d, half_other], cr_main.at[d], cm_s.at[d], cm_r.at[d], dev(z, x, y, 1 - c))

    def make(d):
        a = abuf[...].reshape(4 * 128, KW)
        wt = wbuf[pl.ds(mod(y + d, NY) * 4, 4)].reshape(4 * WC, KW)
        cs_main[d] = lax.dot_general(wt, a, NT, preferred_element_type=F32)
        cm(d).start()

    fori(0, NY, make)

    def hm_in(p):
        src = lax.rem(x * 4 + y + p, 16)
        return rcopy(hmsg.at[0, 0], hrb.at[src], hm_s.at[0], hm_r.at[src], dev(z, x, y, 1 - c))

    gain_in.wait()
    gain2[...] = gain_ref[...].astype(F32).reshape(1, 5120)
    fori(1, 16, lambda p: hm_in(p).wait_recv())
    hlane = lax.broadcasted_iota(jnp.int32, (32, HD), 1)
    hproj = jnp.zeros((32, KW), F32)
    for xs in range(NX):
        tot = hrb[xs * 4].astype(F32)
        for ys in range(1, NY):
            tot += hrb[xs * 4 + ys].astype(F32)
        for j in range(2):
            blk = j * 4 + xs
            piece = jnp.where(hlane < WC, tot[j * 32 : j * 32 + 32, :], 0.0)
            wide = jnp.concatenate([piece, jnp.zeros((32, KW - HD), F32)], axis=1)
            hproj += pltpu.roll(wide, blk * WC, 1) if blk else wide

    def drows(tt):
        return hbuf.at[pl.ds(64, 16), pl.ds(pl.multiple_of(tt * KW, HD), KW)]

    def hrows(xx, tt):
        return hbuf.at[pl.ds(pl.multiple_of(xx * 16, 16), 16), pl.ds(pl.multiple_of(tt * KW, HD), KW)]

    hrows(x, t)[...] = (hres[0:16, :] + hproj[0:16]).astype(BF16)

    def hbc(p, i):
        q = lax.rem(x * 4 + y + p, 16)
        ref = hrows(lax.div(i, 4), lax.rem(i, 4) * NC + c)
        return rcopy(ref, ref, hb_s.at[p], hb_r.at[p], dev(z, lax.div(q, 4), lax.rem(q, 4), c))

    def hcc(p, i, cc):
        ref = hrows(lax.div(i, 4), lax.rem(i, 4) * NC + cc)
        return rcopy(ref, ref, hc_s.at[p], hc_r.at[p], dev(z, x, y, 1 - c))

    def from_(p):
        return lax.rem(x * 4 + y - p + 16, 16)

    def dbc(d, yy):
        ref = drows(yy * NC + c)
        return rcopy(ref, ref, db_s.at[d], db_r.at[d], dev(z, x, mod(y + d, NY), c))

    def dcc(d, yy, cc):
        ref = drows(yy * NC + cc)
        return rcopy(ref, ref, dc_s.at[d], dc_r.at[d], dev(z, x, y, 1 - c))

    fori(1, 16, lambda p: hbc(p, from_(0)).start())
    hcc(0, from_(0), c).start()
    dhid_in.wait()
    dres = (dhid_ref[...].astype(F32) + hproj[16:20]).astype(BF16)
    dout_ref[...] = dres
    drows(t)[...] = jnp.concatenate([dres.astype(F32), jnp.zeros((12, KW), F32)], axis=0).astype(BF16)
    fori(1, NY, lambda d: dbc(d, y).start())
    dcc(0, y, c).start()

    def hfwd(p):
        hbc(p, from_(p)).wait_recv()
        hcc(p, from_(p), c).start()

    fori(1, 16, hfwd)

    def dfwd(d):
        yy = mod(y - d, NY)
        dbc(d, yy).wait_recv()
        dcc(d, yy, c).start()

    fori(1, NY, dfwd)

    fori(0, NY, lambda d: dcc(d, mod(y - d, NY), 1 - c).wait_recv())
    fori(0, 16, lambda p: hcc(p, from_(p), 1 - c).wait_recv())
    hw_copy.wait()

    def chunk(i):
        return pl.ds(pl.multiple_of(i * KW, HD), KW)

    def square(i, acc):
        v = hbuf[:, chunk(i)].astype(F32)
        return acc + jnp.sum(v * v, axis=-1, keepdims=True)

    ssq = lax.fori_loop(0, 8, square, jnp.zeros((80, 1), F32))
    inv = lax.rsqrt(ssq / 5120.0 + EPS)
    vocab = hwbuf.shape[0]

    def logit(i, acc):
        v = hbuf[:, chunk(i)].astype(F32)
        n = (v * inv * gain2[:, chunk(i)]).astype(BF16)
        return acc + lax.dot_general(n, hwbuf[:, chunk(i)], NT, preferred_element_type=F32)

    logits = lax.fori_loop(0, 8, logit, jnp.zeros((80, vocab), F32))
    lm = jnp.max(logits, axis=-1, keepdims=True)
    ll = jnp.sum(jnp.exp(logits - lm), axis=-1, keepdims=True)

    ln = lax.broadcasted_iota(jnp.int32, (80, HD), 1)
    tmat[...] = jnp.zeros_like(tmat)
    tmat[0:80, :] = jnp.where(ln == 0, lm, jnp.where(ln == 1, ll, 0.0))
    me = x * 8 + t
    lsz[z] = tmat[...].T[0:8, :]

    def lzc(d, i):
        return rcopy(lsz.at[i], lsz.at[i], lz_s.at[d], lz_r.at[d], dev(mod(z + d, NZ), x, y, c))

    def lsc(p, i):
        return rcopy(lst.at[i], lst.at[i], ls_s.at[p], ls_r.at[p], plane(p))

    def join(ref, n):
        f = ref.reshape(n * 8, HD)
        ms = f[pl.ds(0, n, stride=8), :]
        lls = f[pl.ds(1, n, stride=8), :]
        top = jnp.max(ms, axis=0, keepdims=True)
        return top, jnp.sum(lls * jnp.exp(ms - top), axis=0, keepdims=True)

    def far(n):
        k = lax.div(n + 1, 2)
        return 8 + k - 2 * k * lax.rem(n, 2)

    fori(0, NZ - 1, lambda n: lzc(far(n), z).start())

    def r_copy(d, xx):
        return rcopy(
            msg.at[d * 4 + xx],
            rbuf.at[x * 4 + y],
            r_s.at[d * 4 + xx],
            r_r.at[x * 4 + y],
            dev(z, xx, mod(y + d, NY), c),
        )

    def finish(d):
        cm(d).wait_recv()
        own = cs_main.at[d, half_mine]
        for xx in range(NX):
            ls = slice(xx * 128, (xx + 1) * 128)
            msg[d * 4 + xx] = (own[:, ls] + cr_main[d, :, ls]).astype(BF16)

    fori(0, NY, finish)

    fori(4, 20, lambda i: away(lambda d, xx: r_copy(d, xx).start())(lax.rem(i, 16)))
    rbuf[x * 4 + y] = msg[x]

    fori(1, NZ, lambda d: lzc(d, mod(z - d, NZ)).wait_recv())
    top, tot = join(lsz, NZ)
    r8 = lax.broadcasted_iota(jnp.int32, (8, HD), 0)
    lst[me] = jnp.where(r8 == 0, top, tot)
    fori(1, 32, lambda p: lsc(p, me).start())

    def r_in(p):
        src = lax.rem(x * 4 + y + p, 16)
        return rcopy(msg.at[0], rbuf.at[src], r_s.at[0], r_r.at[src], dev(z, x, y, 1 - c))

    fori(1, 16, lambda p: r_in(p).wait_recv())
    for xs in range(NX):
        tot = rbuf[xs * 4].astype(F32)
        for ys in range(1, NY):
            tot += rbuf[xs * 4 + ys].astype(F32)
        for j in range(2):
            blk = j * 4 + xs
            big[blk * WC : (blk + 1) * WC, :] = tot[j * WC : (j + 1) * WC, :]
    for h in range(GROUP):
        ls = slice(h * HD, (h + 1) * HD)
        out_ref[:, ls] = (hid_ref[:, ls].astype(F32) + big[ls, :].T).astype(BF16)

    fori(1, 32, lambda p: lsc(p, lax.rem(me - p + 32, 32)).wait_recv())
    top, tot = join(lst, 32)
    tmat[...] = jnp.broadcast_to(top + jnp.log(tot), (HD, HD))
    lse = tmat[...].T[0:80, 0:1]
    lp = logits - lse
    lp_ref[0:4, :] = lp[64:68]
    for i in range(lpad.shape[0]):
        w = min(HD, vocab - i * HD)
        lpad[i, :, 0:w] = lp[:, i * HD : i * HD + w]
    for i in range(lpad.shape[0]):
        w = min(HD, vocab - i * HD)
        for zz in range(NZ):
            part = lpad.at[i][pl.ds(zz, 4, stride=16), :]
            lp_ref[4 + zz * 4 : 8 + zz * 4, i * HD : i * HD + w] = part[:, 0:w]

    def ring(k):
        for j in range(NCH):
            w_right(k, j).wait_send()
            w_left(k, j).wait_send()

    fori(1, 8, ring)
    for j in range(NCH):
        (w_right if j < 3 else w_left)(8, j).wait_send()

    def three(d):
        dx(d).wait_send()
        a_copy(d, x).wait_send()
        lx(d, x).wait_send()
        d1(d, zl).wait_send()
        d2(d, zg).wait_send()
        df(d, x).wait_send()
        dbc(d, y).wait_send()

    fori(1, 4, three)

    def four(d):
        hx(d).wait_send()
        cm(d).wait_send()
        dcc(d, mod(y - d, NY), c).wait_send()

    fori(0, 4, four)

    fori(0, 16, away_head(lambda e, xx: hm(e, xx).wait_send()))
    fori(0, 16, away(lambda d, xx: r_copy(d, xx).wait_send()))

    def fifteen(d):
        gz(d, z).wait_send()
        lzc(d, z).wait_send()

    fori(1, 16, fifteen)
    fori(1, 16, lambda p: hbc(p, from_(0)).wait_send())
    fori(0, 16, lambda p: hcc(p, from_(p), c).wait_send())
    fori(1, 32, lambda p: lsc(p, me).wait_send())


def local(
    prefill_hidden,
    prefill_query_rows,
    prefill_key_value,
    request_prefix_cache,
    prefix_lengths,
    decode_hidden,
    decode_query_rows,
    decode_kv,
    decode_slot_cache,
    cache_lengths,
    slot_table,
    out_weight,
    final_gain,
    head_weight,
):
    vocab = head_weight.shape[1]
    vm = pl.BlockSpec(memory_space=pltpu.VMEM)
    hbm = pl.BlockSpec(memory_space=pltpu.HBM)
    dma = lambda n: pltpu.SemaphoreType.DMA((n,))
    sems = []
    for n in (9 * NCH, 9 * NCH, 4, 4, 4, 4, 4, 4, 4, 16, 4, 16, 16, 16, 16, 4, 4, 32, 16):
        sems += [dma(n), dma(n)]
    return pl.pallas_call(
        kernel,
        out_shape=(
            jax.ShapeDtypeStruct((128, KW), BF16),
            jax.ShapeDtypeStruct((4, KW), BF16),
            jax.ShapeDtypeStruct((68, vocab), F32),
        ),
        in_specs=[hbm] * 14,
        out_specs=(vm, vm, vm),
        scratch_shapes=[
            pltpu.VMEM(head_weight.shape[::-1], BF16),
            pltpu.VMEM((NZ, WC, KW), BF16),
            pltpu.VMEM((NX, 128, KW), BF16),
            pltpu.VMEM((32, HD), F32),
            pltpu.VMEM((4, 16, HD), F32),
            pltpu.VMEM((4, 16, HD), F32),
            pltpu.VMEM((4, 16, HD), F32),
            pltpu.VMEM((4, 16, HD), F32),
            pltpu.VMEM((4, 8, HD), F32),
            pltpu.VMEM((128, KW), BF16),
            pltpu.VMEM((16, KW), F32),
            pltpu.VMEM((16, HD), F32),
            pltpu.VMEM((NZ * 16, HD), F32),
            pltpu.VMEM((16, KW), F32),
            pltpu.VMEM((NY, 2, NX, 64, HD), F32),
            pltpu.VMEM((NY, NX, 64, HD), F32),
            pltpu.VMEM((NY, NX, 64, HD), BF16),
            pltpu.VMEM((16, 64, HD), BF16),
            pltpu.VMEM((4, 320, 512), F32),
            pltpu.VMEM((4, 160, 512), F32),
            pltpu.VMEM((16, 160, HD), BF16),
            pltpu.VMEM((16, 160, HD), BF16),
            pltpu.VMEM((KW, HD), F32),
            pltpu.VMEM((NZ, 16, HD), BF16),
            pltpu.VMEM((80, 5120), BF16),
            pltpu.VMEM((HD, HD), F32),
            pltpu.VMEM((32, 8, HD), F32),
            pltpu.VMEM((NZ, 8, HD), F32),
            pltpu.VMEM((-(-vocab // HD), 80, HD), F32),
            pltpu.VMEM((128, KW), BF16),
            pltpu.VMEM((2, 1, 768, HD), BF16),
            pltpu.VMEM((2, 5, 128, HD), BF16),
            pltpu.SMEM((64,), jnp.int32),
            pltpu.SMEM((4,), jnp.int32),
            pltpu.SMEM((4,), jnp.int32),
            pltpu.VMEM((128, KW), BF16),
            pltpu.VMEM((2, 128, HD), BF16),
            pltpu.VMEM((4, KW), BF16),
            pltpu.VMEM((4, KW), BF16),
            pltpu.VMEM((2, 4, HD), BF16),
            pltpu.VMEM((5120,), BF16),
            pltpu.VMEM((1, 5120), F32),
            dma(14),
            *sems,
        ],
        compiler_params=pltpu.CompilerParams(
            collective_id=0, has_side_effects=True, vmem_limit_bytes=48 * 1024 * 1024
        ),
    )(
        *[
            pltpu.with_memory_space_constraint(a, pltpu.HBM)
            for a in (
                prefix_lengths,
                cache_lengths,
                slot_table,
                prefill_hidden,
                prefill_query_rows,
                prefill_key_value,
                request_prefix_cache,
                decode_hidden,
                decode_query_rows,
                decode_kv,
                decode_slot_cache,
                out_weight.T,
                final_gain,
                head_weight.T,
            )
        ]
    )


def solution(mesh):
    return jax.shard_map(
        local,
        mesh=mesh,
        in_specs=(
            P("seq", "tp"),
            P("seq", "tp"),
            P(None, "seq", "tp"),
            P(None, "seq", None, "tp"),
            P(),
            P(None, "tp"),
            P(None, "tp"),
            P(None, None, "tp"),
            P(None, None, "seq", "tp"),
            P(),
            P(),
            P("tp", "seq"),
            P(),
            P(None, ("seq", "tp")),
        ),
        out_specs=(P("seq", "tp"), P(None, "tp"), P(None, ("seq", "tp"))),
        check_vma=False,
    )
```

```python
import math

import jax
import jax.numpy as jnp
from jax import lax
from jax.experimental import pallas as pl
from jax.experimental.pallas import tpu as pltpu
from jax.sharding import PartitionSpec as P

NEG = -1e30
EPS = 1e-6
NT = (((1,), (1,)), ((), ()))
MESH = pl.DeviceIdType.MESH
F32 = jnp.float32
BF16 = jnp.bfloat16

NX, NY, NZ, NC = 4, 4, 16, 2
NCH = 5
WR = 16
WC = 80
HD = 128
GROUP = 5
KW = 640


def fori(lo, hi, body):
    def step(i, carry):
        body(i)
        return carry

    lax.fori_loop(lo, hi, step, 0)


def mod(a, n):
    return lax.rem(a + n, n)


def kernel(
    prefix_len_hbm,
    cache_len_hbm,
    slot_hbm,
    hid_hbm,
    q_hbm,
    kv_hbm,
    pre_hbm,
    dhid_hbm,
    dq_hbm,
    dkv_hbm,
    dcache_hbm,
    w_hbm,
    gain_hbm,
    hw_hbm,
    out_ref,
    dout_ref,
    lp_ref,
    hwbuf,
    wbuf,
    abuf,
    qd,
    dpart,
    dxb,
    dz1,
    dz2,
    dfin,
    dmat,
    dtmp,
    lrow,
    rows,
    hres,
    h_buf,
    hr_buf,
    hmsg,
    hrb,
    cs_main,
    cr_main,
    msg,
    rbuf,
    big,
    agz,
    hbuf,
    tmat,
    lst,
    lsp,
    lsz,
    lpad,
    qv,
    prev,
    dcv,
    prefix_len_ref,
    cache_len_ref,
    slot_ref,
    hid_ref,
    kv_ref,
    dhid_ref,
    dq_ref,
    dkv_ref,
    gain_ref,
    gain2,
    in_sem,
    wr_s,
    wr_r,
    wl_s,
    wl_r,
    a_s,
    a_r,
    dx_s,
    dx_r,
    d1_s,
    d1_r,
    d2_s,
    d2_r,
    df_s,
    df_r,
    lx_s,
    lx_r,
    hx_s,
    hx_r,
    hm_s,
    hm_r,
    cm_s,
    cm_r,
    r_s,
    r_r,
    gz_s,
    gz_r,
    hb_s,
    hb_r,
    hc_s,
    hc_r,
    db_s,
    db_r,
    dc_s,
    dc_r,
    ls_s,
    ls_r,
    lp_s,
    lp_r,
    lz_s,
    lz_r,
):
    s = lax.axis_index("seq")
    t = lax.axis_index("tp")
    z, x = lax.div(s, NX), lax.rem(s, NX)
    y, c = lax.div(t, NC), lax.rem(t, NC)
    scale = 1.0 / math.sqrt(HD)

    def dev(zz, xx, yy, cc):
        return (zz * NX + xx, yy * NC + cc)

    def rcopy(src, dst, ss, rs, device):
        return pltpu.make_async_remote_copy(
            src_ref=src, dst_ref=dst, send_sem=ss, recv_sem=rs, device_id=device, device_id_type=MESH
        )

    def bring(i, src, dst):
        copy = pltpu.make_async_copy(src, dst, in_sem.at[i])
        copy.start()
        return copy

    w_in = bring(0, w_hbm, wbuf.at[z])

    def far(n):
        k = lax.div(n + 1, 2)
        return 8 + k - 2 * k * lax.rem(n, 2)

    barrier = pltpu.get_barrier_semaphore()

    def plane(p):
        q = lax.rem(x * 4 + y + p, 16)
        return dev(z, lax.div(q, 4), lax.rem(q, 4), c)

    def greet(device):
        pl.semaphore_signal(barrier, inc=1, device_id=device, device_id_type=MESH)

    fori(0, NZ - 1, lambda n: greet(dev(mod(z + far(n), NZ), x, y, c)))
    fori(1, 16, lambda p: greet(plane(p)))
    greet(dev(z, x, y, 1 - c))

    dq_in = bring(1, dq_hbm, dq_ref)
    slot_in = bring(2, slot_hbm, slot_ref)
    clen_in = bring(3, cache_len_hbm, cache_len_ref)
    d_in = bring(4, dcache_hbm, dcv)
    plen_in = bring(5, prefix_len_hbm, prefix_len_ref)
    p_in = bring(6, pre_hbm, prev)
    q_in = bring(7, q_hbm, qv)
    kv_in = bring(8, kv_hbm, kv_ref)
    hid_in = bring(9, hid_hbm, hid_ref)
    dkv_in = bring(10, dkv_hbm, dkv_ref)
    dhid_in = bring(11, dhid_hbm, dhid_ref)
    gain_in = bring(12, gain_hbm, gain_ref)
    hw_copy = bring(13, hw_hbm, hwbuf)
    w_in.wait()
    pl.semaphore_wait(barrier, NZ - 1 + 15 + 1)

    def w_right(k, j):
        b = wbuf.at[mod(z - k + 1, NZ), pl.ds(j * WR, WR)]
        return rcopy(b, b, wr_s.at[k * NCH + j], wr_r.at[k * NCH + j], dev(mod(z + 1, NZ), x, y, c))

    def w_left(k, j):
        b = wbuf.at[mod(z + k - 1, NZ), pl.ds(j * WR, WR)]
        return rcopy(b, b, wl_s.at[k * NCH + j], wl_r.at[k * NCH + j], dev(mod(z - 1, NZ), x, y, c))

    def w_right_in(k, j):
        b = wbuf.at[mod(z - k, NZ), pl.ds(j * WR, WR)]
        return rcopy(b, b, wr_s.at[k * NCH + j], wr_r.at[k * NCH + j], dev(mod(z + 1, NZ), x, y, c))

    def w_left_in(k, j):
        b = wbuf.at[mod(z + k, NZ), pl.ds(j * WR, WR)]
        return rcopy(b, b, wl_s.at[k * NCH + j], wl_r.at[k * NCH + j], dev(mod(z - 1, NZ), x, y, c))

    def w_forward(k):
        def one(j):
            w_right_in(k, j).wait_recv()
            w_right(k + 1, j).start()
            w_left_in(k, j).wait_recv()
            w_left(k + 1, j).start()

        def turn(j):
            w_right_in(7, j).wait_recv()
            w_left_in(7, j).wait_recv()

            @pl.when(j < 3)
            def _():
                w_right(8, j).start()

            @pl.when(j >= 3)
            def _():
                w_left(8, j).start()

        def last(j):
            @pl.when(j < 3)
            def _():
                w_right_in(8, j).wait_recv()

            @pl.when(j >= 3)
            def _():
                w_left_in(8, j).wait_recv()

        fori(0, NCH, one if k < 7 else turn if k == 7 else last)

    def w_first(j):
        w_right(1, j).start()
        w_left(1, j).start()

    fori(0, NCH, w_first)

    qd[...] = jnp.zeros_like(qd)
    dq_in.wait()
    slot_in.wait()
    clen_in.wait()
    dq = dq_ref[...].astype(F32)
    for r in range(4):
        for h in range(GROUP):
            qd[r * 8 + h : r * 8 + h + 1, :] = dq[r : r + 1, h * HD : (h + 1) * HD]
    qall = qd[...].astype(BF16)
    row = lax.broadcasted_iota(jnp.int32, (32, 1), 0)
    rows_slot = jnp.zeros((32, 1), jnp.int32)
    rows_len = jnp.zeros((32, 1), jnp.int32)
    for r in range(4):
        inside = lax.div(row, 8) == r
        rows_slot = jnp.where(inside, slot_ref[r], rows_slot)
        rows_len = jnp.where(inside, cache_len_ref[r], rows_len)
    d_in.wait()
    keys = dcv[0].reshape(5 * 128, HD)
    vals = dcv[1].reshape(5 * 128, HD)
    col = lax.broadcasted_iota(jnp.int32, (32, 640), 1)
    live = (lax.div(col, 128) == rows_slot) & (s * 128 + lax.rem(col, 128) < rows_len)
    sc = lax.dot_general(qall, keys, NT, preferred_element_type=F32) * scale
    sc = jnp.where(live, sc, NEG)
    dm = jnp.max(sc, axis=-1, keepdims=True)
    dw = jnp.where(live, jnp.exp(sc - dm), 0.0)
    dl = jnp.sum(dw, axis=-1, keepdims=True)
    hi = dw.astype(BF16)
    lo = (dw - hi.astype(F32)).astype(BF16)
    do = jnp.dot(hi, vals, preferred_element_type=F32) + jnp.dot(lo, vals, preferred_element_type=F32)
    lane = lax.broadcasted_iota(jnp.int32, (32, HD), 1)
    dstat = jnp.where(lane < 64, dm, dl)
    for r in range(4):
        dpart[r, 0:8, :] = do[r * 8 : r * 8 + 8]
        dpart[r, 8:16, :] = dstat[r * 8 : r * 8 + 8]

    def dx(d):
        xx = mod(x + d, NX)
        return rcopy(dpart.at[xx], dxb.at[x], dx_s.at[d], dx_r.at[d], dev(z, xx, y, c))

    dxb[x] = dpart[x]
    fori(1, NX, lambda d: dx(d).start())

    plen_in.wait()
    p_in.wait()
    q_in.wait()
    kv_in.wait()
    hid_in.wait()
    pe = prefix_len_ref[s]
    kp, ko = prev[0, 0], kv_ref[0]
    vp, vo = prev[1, 0], kv_ref[1]
    n_pre = kp.shape[0]
    live1 = lax.broadcasted_iota(jnp.int32, (128, n_pre), 1) < pe
    live2 = lax.broadcasted_iota(jnp.int32, (128, 128), 1) <= lax.broadcasted_iota(jnp.int32, (128, 128), 0)
    lrow[...] = jnp.zeros_like(lrow)

    def head(h):
        hs = pl.ds(pl.multiple_of(h * HD, HD), HD)
        qh = qv[:, hs]
        s1 = lax.dot_general(qh, kp, NT, preferred_element_type=F32) * scale
        s2 = lax.dot_general(qh, ko, NT, preferred_element_type=F32) * scale
        s1 = jnp.where(live1, s1, NEG)
        s2 = jnp.where(live2, s2, NEG)
        m = jnp.maximum(jnp.max(s1, -1, keepdims=True), jnp.max(s2, -1, keepdims=True))
        p1 = jnp.where(live1, jnp.exp(s1 - m), 0.0)
        p2 = jnp.where(live2, jnp.exp(s2 - m), 0.0)
        total = jnp.sum(p1, -1, keepdims=True) + jnp.sum(p2, -1, keepdims=True)
        o = jnp.dot(p1.astype(BF16), vp, preferred_element_type=F32)
        o += jnp.dot(p2.astype(BF16), vo, preferred_element_type=F32)
        o = (o / total).astype(BF16)
        abuf[x, :, hs] = o
        lrow[pl.ds(h, 1), :] = o.astype(F32)[127:128, :]
        lrow[pl.ds(8 + h, 1), :] = hid_ref[:, hs].astype(F32)[127:128, :]


    def merge(ref):
        os = [ref[i, 0:8, :] for i in range(4)]
        st = [ref[i, 8:16, :] for i in range(4)]
        ms = [a[:, 0:1] for a in st]
        lls = [a[:, 64:65] for a in st]
        m = jnp.maximum(jnp.maximum(ms[0], ms[1]), jnp.maximum(ms[2], ms[3]))
        o, l = 0.0, 0.0
        for i in range(4):
            f = jnp.exp(ms[i] - m)
            o = o + os[i] * f
            l = l + lls[i] * f
        return o, m, l

    lane8 = lax.broadcasted_iota(jnp.int32, (8, HD), 1)

    def dx_in(d):
        return rcopy(dpart.at[x], dxb.at[mod(x - d, NX)], dx_s.at[d], dx_r.at[d], dev(z, mod(x + d, NX), y, c))

    zl, zg = lax.rem(z, 4), lax.div(z, 4)
    def heads(h):
        head(h)

        @pl.when(h == 2)
        def _():
            w_forward(1)

    fori(0, GROUP, heads)
    fori(1, NX, lambda d: dx_in(d).wait_recv())
    o, m, l = merge(dxb)
    dz1[zl, 0:8, :] = o
    dz1[zl, 8:16, :] = jnp.where(lane8 < 64, m, l)

    def d1(d, slot):
        return rcopy(dz1.at[slot], dz1.at[slot], d1_s.at[d], d1_r.at[d], dev(zg * 4 + mod(zl + d, 4), x, y, c))

    fori(1, 4, lambda d: d1(d, zl).start())

    def a_copy(d, src):
        return rcopy(abuf.at[src], abuf.at[src], a_s.at[d], a_r.at[d], dev(z, mod(x + d, NX), y, c))

    def gz(d, slot):
        return rcopy(agz.at[slot], agz.at[slot], gz_s.at[d], gz_r.at[d], dev(mod(z + d, NZ), x, y, c))

    agz[z] = lrow[...].astype(BF16)
    fori(0, NZ - 1, lambda n: gz(far(n), z).start())
    w_forward(2)
    fori(1, NX, lambda d: a_copy(d, x).start())
    fori(1, 4, lambda d: d1(d, mod(zl - d, 4)).wait_recv())
    o, m, l = merge(dz1)
    dz2[zg, 0:8, :] = o
    dz2[zg, 8:16, :] = jnp.where(lane8 < 64, m, l)

    def d2(d, slot):
        return rcopy(dz2.at[slot], dz2.at[slot], d2_s.at[d], d2_r.at[d], dev(mod(zg + d, 4) * 4 + zl, x, y, c))

    fori(1, 4, lambda d: d2(d, zg).start())
    w_forward(3)
    w_forward(4)
    w_forward(5)

    fori(1, NZ, lambda d: gz(d, mod(z - d, NZ)).wait_recv())
    for i in range(NZ):
        rows[i * 16 : i * 16 + 16, :] = agz[i].astype(F32)
    mine16 = pl.ds(pl.multiple_of(x * 32, 16), 16)
    for h in range(GROUP):
        hs = slice(h * HD, (h + 1) * HD)
        dmat[mine16, hs] = rows[pl.ds(h, NZ, stride=16), :].astype(BF16)
        hres[0:16, hs] = rows[pl.ds(8 + h, NZ, stride=16), :]

    def lx(d, xx):
        ref = dmat.at[pl.ds(pl.multiple_of(xx * 32, 16), 16)]
        return rcopy(ref, ref, lx_s.at[d], lx_r.at[d], dev(z, mod(x + d, NX), y, c))

    fori(1, NX, lambda d: lx(d, x).start())
    w_forward(6)
    fori(1, 4, lambda d: d2(d, mod(zg - d, 4)).wait_recv())
    o, m, l = merge(dz2)
    dkv_in.wait()
    row4 = lax.broadcasted_iota(jnp.int32, (4, HD), 0)
    own_k = jnp.sum(jnp.where(row4 == x, dkv_ref[0].astype(F32), 0.0), axis=0, keepdims=True)
    own_v = jnp.sum(jnp.where(row4 == x, dkv_ref[1].astype(F32), 0.0), axis=0, keepdims=True)
    own_q = qd[pl.ds(pl.multiple_of(x * 8, 8), 8), :]
    own_s = jnp.sum(own_q * own_k, axis=-1, keepdims=True) * scale
    m2 = jnp.maximum(m, own_s)
    f1, f2 = jnp.exp(m - m2), jnp.exp(own_s - m2)
    dfin[x] = (o * f1 + own_v * f2) / (l * f1 + f2)

    def df(d, slot):
        return rcopy(dfin.at[slot], dfin.at[slot], df_s.at[d], df_r.at[d], dev(z, mod(x + d, NX), y, c))

    fori(1, NX, lambda d: df(d, x).start())
    w_forward(7)
    fori(1, NX, lambda d: a_copy(d, mod(x - d, NX)).wait_recv())
    fori(1, NX, lambda d: lx(d, mod(x - d, NX)).wait_recv())
    fori(1, NX, lambda d: df(d, mod(x - d, NX)).wait_recv())
    dtmp[...] = jnp.zeros_like(dtmp)
    for r in range(4):
        for h in range(GROUP):
            dtmp[r : r + 1, h * HD : (h + 1) * HD] = dfin[r, h : h + 1, :]
    for xx in range(NX):
        dmat[xx * 32 + 16 : xx * 32 + 32, :] = dtmp[...].astype(BF16)
    h_buf[...] = jnp.zeros_like(h_buf)

    def head_product(e, i):
        p = lax.dot_general(dmat[...], wbuf[mod(zg + e, NY) * 4 + i], NT, preferred_element_type=F32)
        half = pl.ds(pl.multiple_of(lax.rem(i, 2) * 32, 32), 32)
        for xx in range(NX):
            h_buf[e, lax.div(i, 2), xx, half, 0:WC] = p[xx * 32 : xx * 32 + 32]

    def hx(e):
        return rcopy(h_buf.at[e, 1 - c], hr_buf.at[e], hx_s.at[e], hx_r.at[e], dev(z, x, y, 1 - c))

    def head_group(e):
        fori(0, 4, lambda i: head_product(e, i))
        hx(e).start()

    def hm(e, xx):
        return rcopy(
            hmsg.at[e, xx],
            hrb.at[x * 4 + y],
            hm_s.at[e * 4 + xx],
            hm_r.at[x * 4 + y],
            dev(z, xx, mod(zg + e, NY), c),
        )

    def away_head(fn):
        def each(e, xx):
            @pl.when((mod(zg + e, NY) != y) | (xx != x))
            def _():
                fn(e, xx)

        return lambda i: each(lax.div(i, 4), lax.rem(i, 4))

    def head_send(e):
        hx(e).wait_recv()
        hmsg[e] = (h_buf[e, c] + hr_buf[e]).astype(BF16)
        fori(e * 4, e * 4 + 4, away_head(lambda e, xx: hm(e, xx).start()))

    def head_step(i):
        @pl.when(i == 3)
        def _():
            w_forward(8)

        head_group(i + lax.div(i, 2) - 2 * lax.div(i, 3))

    fori(0, 4, head_step)
    fori(0, 4, lambda i: head_send(i + lax.div(i, 2) - 2 * lax.div(i, 3)))
    hrb[x * 4 + y] = hmsg[mod(y - zg, NY), x]

    def away(fn):
        def each(d, xx):
            @pl.when((d != 0) | (xx != x))
            def _():
                fn(d, xx)

        return lambda i: each(lax.div(i, 4), lax.rem(i, 4))

    half_other = pl.ds(pl.multiple_of((1 - c) * 160, 8), 160)
    half_mine = pl.ds(pl.multiple_of(c * 160, 8), 160)

    def cm(d):
        return rcopy(cs_main.at[d, half_other], cr_main.at[d], cm_s.at[d], cm_r.at[d], dev(z, x, y, 1 - c))

    def make(d):
        a = abuf[...].reshape(4 * 128, KW)
        wt = wbuf[pl.ds(mod(y + d, NY) * 4, 4)].reshape(4 * WC, KW)
        cs_main[d] = lax.dot_general(wt, a, NT, preferred_element_type=F32)
        cm(d).start()

    fori(0, NY, make)

    def hm_in(p):
        src = lax.rem(x * 4 + y + p, 16)
        return rcopy(hmsg.at[0, 0], hrb.at[src], hm_s.at[0], hm_r.at[src], dev(z, x, y, 1 - c))

    gain_in.wait()
    gain2[...] = gain_ref[...].astype(F32).reshape(1, 5120)
    fori(1, 16, lambda p: hm_in(p).wait_recv())
    hlane = lax.broadcasted_iota(jnp.int32, (32, HD), 1)
    hproj = jnp.zeros((32, KW), F32)
    for xs in range(NX):
        tot = hrb[xs * 4].astype(F32)
        for ys in range(1, NY):
            tot += hrb[xs * 4 + ys].astype(F32)
        for j in range(2):
            blk = j * 4 + xs
            piece = jnp.where(hlane < WC, tot[j * 32 : j * 32 + 32, :], 0.0)
            wide = jnp.concatenate([piece, jnp.zeros((32, KW - HD), F32)], axis=1)
            hproj += pltpu.roll(wide, blk * WC, 1) if blk else wide

    def drows(tt):
        return hbuf.at[pl.ds(64, 16), pl.ds(pl.multiple_of(tt * KW, HD), KW)]

    def hrows(xx, tt):
        return hbuf.at[pl.ds(pl.multiple_of(xx * 16, 16), 16), pl.ds(pl.multiple_of(tt * KW, HD), KW)]

    hrows(x, t)[...] = (hres[0:16, :] + hproj[0:16]).astype(BF16)

    def hbc(p, i):
        q = lax.rem(x * 4 + y + p, 16)
        ref = hrows(lax.div(i, 4), lax.rem(i, 4) * NC + c)
        return rcopy(ref, ref, hb_s.at[p], hb_r.at[p], dev(z, lax.div(q, 4), lax.rem(q, 4), c))

    def hcc(p, i, cc):
        ref = hrows(lax.div(i, 4), lax.rem(i, 4) * NC + cc)
        return rcopy(ref, ref, hc_s.at[p], hc_r.at[p], dev(z, x, y, 1 - c))

    def from_(p):
        return lax.rem(x * 4 + y - p + 16, 16)

    def dbc(d, yy):
        ref = drows(yy * NC + c)
        return rcopy(ref, ref, db_s.at[d], db_r.at[d], dev(z, x, mod(y + d, NY), c))

    def dcc(d, yy, cc):
        ref = drows(yy * NC + cc)
        return rcopy(ref, ref, dc_s.at[d], dc_r.at[d], dev(z, x, y, 1 - c))

    fori(1, 16, lambda p: hbc(p, from_(0)).start())
    hcc(0, from_(0), c).start()
    dhid_in.wait()
    dres = (dhid_ref[...].astype(F32) + hproj[16:20]).astype(BF16)
    dout_ref[...] = dres
    drows(t)[...] = jnp.concatenate([dres.astype(F32), jnp.zeros((12, KW), F32)], axis=0).astype(BF16)
    fori(1, NY, lambda d: dbc(d, y).start())
    dcc(0, y, c).start()

    def hfwd(p):
        hbc(p, from_(p)).wait_recv()
        hcc(p, from_(p), c).start()

    fori(1, 16, hfwd)

    def dfwd(d):
        yy = mod(y - d, NY)
        dbc(d, yy).wait_recv()
        dcc(d, yy, c).start()

    fori(1, NY, dfwd)

    fori(0, NY, lambda d: dcc(d, mod(y - d, NY), 1 - c).wait_recv())
    fori(0, 16, lambda p: hcc(p, from_(p), 1 - c).wait_recv())
    hw_copy.wait()

    def chunk(i):
        return pl.ds(pl.multiple_of(i * KW, HD), KW)

    def square(i, acc):
        v = hbuf[:, chunk(i)].astype(F32)
        return acc + jnp.sum(v * v, axis=-1, keepdims=True)

    ssq = lax.fori_loop(0, 8, square, jnp.zeros((80, 1), F32))
    inv = lax.rsqrt(ssq / 5120.0 + EPS)
    vocab = hwbuf.shape[0]

    def logit(i, acc):
        v = hbuf[:, chunk(i)].astype(F32)
        n = (v * inv * gain2[:, chunk(i)]).astype(BF16)
        return acc + lax.dot_general(n, hwbuf[:, chunk(i)], NT, preferred_element_type=F32)

    logits = lax.fori_loop(0, 8, logit, jnp.zeros((80, vocab), F32))
    lm = jnp.max(logits, axis=-1, keepdims=True)
    ll = jnp.sum(jnp.exp(logits - lm), axis=-1, keepdims=True)

    ln = lax.broadcasted_iota(jnp.int32, (80, HD), 1)
    tmat[...] = jnp.zeros_like(tmat)
    tmat[0:80, :] = jnp.where(ln == 0, lm, jnp.where(ln == 1, ll, 0.0))
    me = x * 4 + y
    lsz[z] = tmat[...].T[0:8, :]

    def lzc(d, i):
        return rcopy(lsz.at[i], lsz.at[i], lz_s.at[d], lz_r.at[d], dev(mod(z + d, NZ), x, y, c))

    def lsc(p, i):
        return rcopy(lst.at[i], lst.at[i], ls_s.at[p], ls_r.at[p], plane(p))

    def join(ref, n):
        f = ref.reshape(n * 8, HD)
        ms = f[pl.ds(0, n, stride=8), :]
        lls = f[pl.ds(1, n, stride=8), :]
        top = jnp.max(ms, axis=0, keepdims=True)
        return top, jnp.sum(lls * jnp.exp(ms - top), axis=0, keepdims=True)

    fori(0, NZ - 1, lambda n: lzc(far(n), z).start())

    def r_copy(d, xx):
        return rcopy(
            msg.at[d * 4 + xx],
            rbuf.at[x * 4 + y],
            r_s.at[d * 4 + xx],
            r_r.at[x * 4 + y],
            dev(z, xx, mod(y + d, NY), c),
        )

    def finish(d):
        cm(d).wait_recv()
        own = cs_main.at[d, half_mine]
        for xx in range(NX):
            ls = slice(xx * 128, (xx + 1) * 128)
            msg[d * 4 + xx] = (own[:, ls] + cr_main[d, :, ls]).astype(BF16)

    fori(0, NY, finish)

    fori(4, 20, lambda i: away(lambda d, xx: r_copy(d, xx).start())(lax.rem(i, 16)))
    rbuf[x * 4 + y] = msg[x]

    fori(1, NZ, lambda d: lzc(d, mod(z - d, NZ)).wait_recv())
    top, tot = join(lsz, NZ)
    r8 = lax.broadcasted_iota(jnp.int32, (8, HD), 0)
    lsp[c] = jnp.where(r8 == 0, top, tot)

    def lpc(i):
        return rcopy(lsp.at[i], lsp.at[i], lp_s.at[0], lp_r.at[0], dev(z, x, y, 1 - c))

    lpc(c).start()
    lpc(1 - c).wait_recv()
    top, tot = join(lsp, 2)
    lst[me] = jnp.where(r8 == 0, top, tot)
    fori(1, 16, lambda p: lsc(p, me).start())

    def r_in(p):
        src = lax.rem(x * 4 + y + p, 16)
        return rcopy(msg.at[0], rbuf.at[src], r_s.at[0], r_r.at[src], dev(z, x, y, 1 - c))

    fori(1, 16, lambda p: r_in(p).wait_recv())
    for xs in range(NX):
        tot = rbuf[xs * 4].astype(F32)
        for ys in range(1, NY):
            tot += rbuf[xs * 4 + ys].astype(F32)
        for j in range(2):
            blk = j * 4 + xs
            big[blk * WC : (blk + 1) * WC, :] = tot[j * WC : (j + 1) * WC, :]
    for h in range(GROUP):
        ls = slice(h * HD, (h + 1) * HD)
        out_ref[:, ls] = (hid_ref[:, ls].astype(F32) + big[ls, :].T).astype(BF16)

    fori(1, 16, lambda p: lsc(p, from_(p)).wait_recv())
    top, tot = join(lst, 16)
    tmat[...] = jnp.broadcast_to(top + jnp.log(tot), (HD, HD))
    lse = tmat[...].T[0:80, 0:1]
    lp = logits - lse
    lp_ref[0:4, :] = lp[64:68]
    for i in range(lpad.shape[0]):
        w = min(HD, vocab - i * HD)
        lpad[i, :, 0:w] = lp[:, i * HD : i * HD + w]
    for i in range(lpad.shape[0]):
        w = min(HD, vocab - i * HD)
        for zz in range(NZ):
            part = lpad.at[i][pl.ds(zz, 4, stride=16), :]
            lp_ref[4 + zz * 4 : 8 + zz * 4, i * HD : i * HD + w] = part[:, 0:w]

    def ring(k):
        for j in range(NCH):
            w_right(k, j).wait_send()
            w_left(k, j).wait_send()

    fori(1, 8, ring)
    for j in range(NCH):
        (w_right if j < 3 else w_left)(8, j).wait_send()

    def three(d):
        dx(d).wait_send()
        a_copy(d, x).wait_send()
        lx(d, x).wait_send()
        d1(d, zl).wait_send()
        d2(d, zg).wait_send()
        df(d, x).wait_send()
        dbc(d, y).wait_send()

    fori(1, 4, three)

    def four(d):
        hx(d).wait_send()
        cm(d).wait_send()
        dcc(d, mod(y - d, NY), c).wait_send()

    fori(0, 4, four)

    fori(0, 16, away_head(lambda e, xx: hm(e, xx).wait_send()))
    fori(0, 16, away(lambda d, xx: r_copy(d, xx).wait_send()))

    def fifteen(d):
        gz(d, z).wait_send()
        lzc(d, z).wait_send()

    fori(1, 16, fifteen)
    fori(1, 16, lambda p: hbc(p, from_(0)).wait_send())
    fori(0, 16, lambda p: hcc(p, from_(p), c).wait_send())
    fori(1, 16, lambda p: lsc(p, me).wait_send())
    lpc(c).wait_send()


def local(
    prefill_hidden,
    prefill_query_rows,
    prefill_key_value,
    request_prefix_cache,
    prefix_lengths,
    decode_hidden,
    decode_query_rows,
    decode_kv,
    decode_slot_cache,
    cache_lengths,
    slot_table,
    out_weight,
    final_gain,
    head_weight,
):
    vocab = head_weight.shape[1]
    vm = pl.BlockSpec(memory_space=pltpu.VMEM)
    hbm = pl.BlockSpec(memory_space=pltpu.HBM)
    dma = lambda n: pltpu.SemaphoreType.DMA((n,))
    sems = []
    for n in (9 * NCH, 9 * NCH, 4, 4, 4, 4, 4, 4, 4, 16, 4, 16, 16, 16, 16, 4, 4, 16, 1, 16):
        sems += [dma(n), dma(n)]
    return pl.pallas_call(
        kernel,
        out_shape=(
            jax.ShapeDtypeStruct((128, KW), BF16),
            jax.ShapeDtypeStruct((4, KW), BF16),
            jax.ShapeDtypeStruct((68, vocab), F32),
        ),
        in_specs=[hbm] * 14,
        out_specs=(vm, vm, vm),
        scratch_shapes=[
            pltpu.VMEM(head_weight.shape[::-1], BF16),
            pltpu.VMEM((NZ, WC, KW), BF16),
            pltpu.VMEM((NX, 128, KW), BF16),
            pltpu.VMEM((32, HD), F32),
            pltpu.VMEM((4, 16, HD), F32),
            pltpu.VMEM((4, 16, HD), F32),
            pltpu.VMEM((4, 16, HD), F32),
            pltpu.VMEM((4, 16, HD), F32),
            pltpu.VMEM((4, 8, HD), F32),
            pltpu.VMEM((128, KW), BF16),
            pltpu.VMEM((16, KW), F32),
            pltpu.VMEM((16, HD), F32),
            pltpu.VMEM((NZ * 16, HD), F32),
            pltpu.VMEM((16, KW), F32),
            pltpu.VMEM((NY, 2, NX, 64, HD), F32),
            pltpu.VMEM((NY, NX, 64, HD), F32),
            pltpu.VMEM((NY, NX, 64, HD), BF16),
            pltpu.VMEM((16, 64, HD), BF16),
            pltpu.VMEM((4, 320, 512), F32),
            pltpu.VMEM((4, 160, 512), F32),
            pltpu.VMEM((16, 160, HD), BF16),
            pltpu.VMEM((16, 160, HD), BF16),
            pltpu.VMEM((KW, HD), F32),
            pltpu.VMEM((NZ, 16, HD), BF16),
            pltpu.VMEM((80, 5120), BF16),
            pltpu.VMEM((HD, HD), F32),
            pltpu.VMEM((16, 8, HD), F32),
            pltpu.VMEM((2, 8, HD), F32),
            pltpu.VMEM((NZ, 8, HD), F32),
            pltpu.VMEM((-(-vocab // HD), 80, HD), F32),
            pltpu.VMEM((128, KW), BF16),
            pltpu.VMEM((2, 1, 768, HD), BF16),
            pltpu.VMEM((2, 5, 128, HD), BF16),
            pltpu.SMEM((64,), jnp.int32),
            pltpu.SMEM((4,), jnp.int32),
            pltpu.SMEM((4,), jnp.int32),
            pltpu.VMEM((128, KW), BF16),
            pltpu.VMEM((2, 128, HD), BF16),
            pltpu.VMEM((4, KW), BF16),
            pltpu.VMEM((4, KW), BF16),
            pltpu.VMEM((2, 4, HD), BF16),
            pltpu.VMEM((5120,), BF16),
            pltpu.VMEM((1, 5120), F32),
            dma(14),
            *sems,
        ],
        compiler_params=pltpu.CompilerParams(
            collective_id=0, has_side_effects=True, vmem_limit_bytes=48 * 1024 * 1024
        ),
    )(
        *[
            pltpu.with_memory_space_constraint(a, pltpu.HBM)
            for a in (
                prefix_lengths,
                cache_lengths,
                slot_table,
                prefill_hidden,
                prefill_query_rows,
                prefill_key_value,
                request_prefix_cache,
                decode_hidden,
                decode_query_rows,
                decode_kv,
                decode_slot_cache,
                out_weight.T,
                final_gain,
                head_weight.T,
            )
        ]
    )


def solution(mesh):
    return jax.shard_map(
        local,
        mesh=mesh,
        in_specs=(
            P("seq", "tp"),
            P("seq", "tp"),
            P(None, "seq", "tp"),
            P(None, "seq", None, "tp"),
            P(),
            P(None, "tp"),
            P(None, "tp"),
            P(None, None, "tp"),
            P(None, None, "seq", "tp"),
            P(),
            P(),
            P("tp", "seq"),
            P(),
            P(None, ("seq", "tp")),
        ),
        out_specs=(P("seq", "tp"), P(None, "tp"), P(None, ("seq", "tp"))),
        check_vma=False,
    )
```
